512 devices in a mesh: dp: 32 (over x_lo, z), ctx: 16 (over x_hi, y, core).
Axes of the slice: x: 4 (x_hi: 2, x_lo: 2; x = x_hi * 2 + x_lo), y: 4, z: 16, core: 2. Of those that a mesh axis runs over, the one named last changes fastest.
Arguments:
- hidden_in: bfloat16 [32, 2048, 2560], P('dp', 'ctx'), may hold values from -6 to 6
- queries: bfloat16 [32, 2048, 2048], P('dp', 'ctx'), may hold values from -6 to 6
- keys_values: bfloat16 [32, 2048, 1024], P('dp', 'ctx'), may hold values from -6 to 6
- attn_out: bfloat16 [32, 2048, 2048], P('dp', 'ctx'), may hold values from -2 to 2
- out_grad: bfloat16 [32, 2048, 2048], P('dp', 'ctx'), may hold values from -6 to 6
- log_norms: float32 [32, 16, 2048], P('dp', None, 'ctx')
- proj_in: bfloat16 [2560, 64], replicated, may hold values from -0.125 to 0.125
- proj_q: bfloat16 [2048, 64], replicated, may hold values from -0.125 to 0.125
- proj_k: bfloat16 [512, 64], replicated, may hold values from -0.25 to 0.25
- proj_v: bfloat16 [512, 64], replicated, may hold values from -0.25 to 0.25
- query_docs: int32 [8], replicated, may hold values from 0 to 31
Outputs:
- unit_grads: float32 [32, 12288], P('dp')
- scores: float32 [32, 8], P('dp')
The draws below stay inside these ranges and needn't reach their ends.
All inputs are finite; a program needn't handle non-finite values.
Results may differ from the reference program's by a relative error of at most 0.0041.
Values may be sent and summed in bfloat16 or wider, within the bound.
No kernel may reach another device: no remote copies, remote signals or barrier semaphores. Data moves between devices by JAX's collectives and lax.ppermute only.
A program may use at most 128 MiB of HBM per device.

```python
import jax
import jax.numpy as jnp
from jax import lax

D = 2560
HEADS = 16
KV_HEADS = 4
HEAD_DIM = 128
RANK = 64
NQ = 8
TOKENS = 2048
DOCS = 32


def sample_part(key, shape):
    normal_part = jax.random.truncated_normal(key, -4.0, 4.0, shape, jnp.float32)
    return normal_part


def mixed_field(key, width, spread):
    common = sample_part(jax.random.fold_in(key, 1), (1, TOKENS, width))
    own_part = sample_part(jax.random.fold_in(key, 2), (DOCS, TOKENS, width))
    return (spread * (0.92 * common + 0.392 * own_part)).astype(jnp.bfloat16)


def draw_hidden_in(key, part):
    key = jax.random.fold_in(key, 21)
    return mixed_field(key, D, 1.0)


def draw_queries(key, part):
    key = jax.random.fold_in(key, 22)
    return mixed_field(key, HEADS * HEAD_DIM, 1.0)


def draw_keys_values(key, part):
    key = jax.random.fold_in(key, 23)
    return mixed_field(key, 2 * KV_HEADS * HEAD_DIM, 1.0)


def draw_attn_out(key, part):
    key = jax.random.fold_in(key, 24)
    return mixed_field(key, HEADS * HEAD_DIM, 0.3)


def draw_out_grad(key, part):
    key = jax.random.fold_in(key, 25)
    return mixed_field(key, HEADS * HEAD_DIM, 1.0)


def draw_log_norms(key, part):
    key = jax.random.fold_in(key, 11)
    shape = (DOCS, HEADS, TOKENS)
    position = lax.broadcasted_iota(jnp.float32, shape, 2)
    noise = jax.random.uniform(key, shape, jnp.float32, -0.5, 0.5)
    return jnp.log(position + 1.0) + 0.5 + noise


def place_ends(entries, rng, low, largest):
    index_at = [jax.random.randint(jax.random.fold_in(rng, axis), (), 0, length) for axis, length in enumerate(entries.shape)]
    longest = entries.shape.index(max(entries.shape))
    beside = index_at[:longest] + [(index_at[longest] + 1) % entries.shape[longest]] + index_at[longest + 1:]
    return entries.at[tuple(index_at)].set(low).at[tuple(beside)].set(largest)


def gaussian(stream_key, shape, scale, limit, kind=jnp.bfloat16):
    result = scale * jax.random.normal(stream_key, shape, jnp.float32)
    return jnp.clip(result, min=-limit, max=limit).astype(kind)


def setup_inputs(seed: int = 0) -> dict:
    key_of = jax.random.split(jax.random.key(seed), 12)
    return {
        "hidden_in": draw_hidden_in(jax.random.fold_in(key_of[11], 71), 0),
        "queries": draw_queries(jax.random.fold_in(key_of[11], 71), 0),
        "keys_values": draw_keys_values(jax.random.fold_in(key_of[11], 71), 0),
        "attn_out": draw_attn_out(jax.random.fold_in(key_of[11], 71), 0),
        "out_grad": draw_out_grad(jax.random.fold_in(key_of[11], 71), 0),
        "log_norms": draw_log_norms(jax.random.fold_in(key_of[11], 71), 0),
        "proj_in": gaussian(key_of[6], (D, RANK), D ** -0.5, 0.125),
        "proj_q": gaussian(key_of[7], (HEADS * HEAD_DIM, RANK), (HEADS * HEAD_DIM) ** -0.5, 0.125),
        "proj_k": gaussian(key_of[8], (KV_HEADS * HEAD_DIM, RANK), (KV_HEADS * HEAD_DIM) ** -0.5, 0.25),
        "proj_v": gaussian(key_of[9], (KV_HEADS * HEAD_DIM, RANK), (KV_HEADS * HEAD_DIM) ** -0.5, 0.25),
        "query_docs": place_ends(jax.random.randint(key_of[10], (NQ,), 0, DOCS), jax.random.fold_in(key_of[10], 1), 0, DOCS - 1).astype(jnp.int32),
    }


def one_document(x, q, kv, o, dout, lse, proj_in, proj_q, proj_k, proj_v):
    group = HEADS // KV_HEADS
    scale = HEAD_DIM ** (-0.5)
    pos = jnp.arange(TOKENS, dtype=jnp.int32)
    visible = pos[None, :] <= pos[:, None]
    q_heads = q.reshape(TOKENS, HEADS, HEAD_DIM).transpose(1, 0, 2)
    d_heads = dout.reshape(TOKENS, HEADS, HEAD_DIM).transpose(1, 0, 2)
    o_heads = o.reshape(TOKENS, HEADS, HEAD_DIM).transpose(1, 0, 2)
    keys = kv[:, :KV_HEADS * HEAD_DIM].reshape(TOKENS, KV_HEADS, HEAD_DIM).transpose(1, 0, 2)
    values = kv[:, KV_HEADS * HEAD_DIM:].reshape(TOKENS, KV_HEADS, HEAD_DIM).transpose(1, 0, 2)
    kv_index = jnp.arange(HEADS, dtype=jnp.int32) // group

    def per_head(args):
        qh, dh, oh, lh, kidx = args
        kh = keys[kidx]
        vh = values[kidx]
        scores_h = jnp.dot(qh, kh.T, preferred_element_type=jnp.float32) * scale
        probs = jnp.exp(jnp.where(visible, scores_h - lh[:, None], -1e+30))
        dprobs = jnp.dot(dh, vh.T, preferred_element_type=jnp.float32)
        delta = lax.optimization_barrier(jnp.sum(dh.astype(jnp.float32) * oh.astype(jnp.float32), axis=1))
        dscores = probs * (dprobs - delta[:, None])
        probs_b = probs.astype(jnp.bfloat16)
        dscores_b = dscores.astype(jnp.bfloat16)
        grad_q = jnp.dot(dscores_b, kh, preferred_element_type=jnp.float32) * scale
        grad_k = jnp.dot(dscores_b.T, qh, preferred_element_type=jnp.float32) * scale
        grad_v = jnp.dot(probs_b.T, dh, preferred_element_type=jnp.float32)
        return (grad_q, grad_k, grad_v)
    grad_q, grad_k, grad_v = lax.map(per_head, (q_heads, d_heads, o_heads, lse, kv_index))
    grad_q = grad_q.transpose(1, 0, 2).reshape(TOKENS, HEADS * HEAD_DIM)
    grad_k = grad_k.reshape(KV_HEADS, group, TOKENS, HEAD_DIM).sum(axis=1).transpose(1, 0, 2).reshape(TOKENS, KV_HEADS * HEAD_DIM)
    grad_v = grad_v.reshape(KV_HEADS, group, TOKENS, HEAD_DIM).sum(axis=1).transpose(1, 0, 2).reshape(TOKENS, KV_HEADS * HEAD_DIM)
    high = lax.Precision.HIGHEST
    inputs_p = jnp.dot(x, proj_in, preferred_element_type=jnp.float32).astype(jnp.bfloat16)
    outs_p = jnp.concatenate([jnp.dot(grad_q, proj_q.astype(jnp.float32), precision=high), jnp.dot(grad_k, proj_k.astype(jnp.float32), precision=high), jnp.dot(grad_v, proj_v.astype(jnp.float32), precision=high)], axis=1)
    doc_grad = jnp.dot(inputs_p.astype(jnp.float32).T, outs_p, precision=high).reshape(-1)
    return doc_grad / jnp.sqrt(jnp.mean(doc_grad * doc_grad) + 1e-06)

def reference(hidden_in, queries, keys_values, attn_out, out_grad, log_norms, proj_in, proj_q, proj_k, proj_v, query_docs):

    def per_doc(args):
        x, q, kv, o, dout, lse = args
        return one_document(x, q, kv, o, dout, lse, proj_in, proj_q, proj_k, proj_v)
    unit_grads = lax.map(per_doc, (hidden_in, queries, keys_values, attn_out, out_grad, log_norms))
    chosen = unit_grads[query_docs.astype(jnp.int32)]
    scores = jnp.dot(unit_grads, chosen.T, precision=lax.Precision.HIGHEST) / (3.0 * RANK * RANK)
    return (unit_grads, scores)
```

```python
import functools
import math

import jax
import jax.numpy as jnp
from jax import lax
from jax.experimental import pallas as pl
from jax.experimental.pallas import tpu as pltpu
from jax.sharding import PartitionSpec as P

KV_HEADS = 4
HEAD_DIM = 128
RANK = 64
LANES = 128
SCALE = HEAD_DIM ** (-0.5)
F32 = jnp.float32
BF16 = jnp.bfloat16
VMEM = pl.BlockSpec(memory_space=pltpu.VMEM)
SMEM = pl.BlockSpec(memory_space=pltpu.SMEM)

Q_AT, D_AT, K_AT, V_AT, X_AT, WIDE = 0, 256, 512, 640, 768, 896


def nt(a, b):
    return lax.dot_general(a, b, (((1,), (1,)), ((), ())), preferred_element_type=F32)


def tn(a, b):
    return lax.dot_general(a, b, (((0,), (0,)), ((), ())), preferred_element_type=F32)


def nn(a, b):
    return jnp.dot(a, b, preferred_element_type=F32)


def split2(a):
    high = a.astype(BF16)
    return high, (a - high.astype(F32)).astype(BF16)


def lane_of(shape):
    return lax.broadcasted_iota(jnp.int32, shape, len(shape) - 1)


def row_of(shape):
    return lax.broadcasted_iota(jnp.int32, shape, len(shape) - 2)


def message_kernel(h_ref, q_ref, kv_ref, o_ref, d_ref, lse_ref, pin_ref, msg_ref):
    tok = q_ref.shape[0]
    heads = lse_ref.shape[0]
    chips = heads // 2
    group = heads // KV_HEADS
    x = nn(h_ref[...], pin_ref[...])
    x = jnp.concatenate([x, jnp.zeros((tok, LANES - RANK), F32)], axis=1)
    lse = jnp.concatenate([lse_ref[...], jnp.zeros((LANES - heads, tok), F32)], axis=0)
    terms = lse.T * (-1.0 / SCALE)
    lane = lane_of((tok, LANES))
    for h in range(heads):
        cols = slice(h * HEAD_DIM, (h + 1) * HEAD_DIM)
        prod = d_ref[:, cols].astype(F32) * o_ref[:, cols].astype(F32)
        delta = jnp.sum(prod, axis=1, keepdims=True)
        terms = jnp.where(lane == heads + h, -delta, terms)
    high, rest = terms.astype(BF16), None
    rest = terms - high.astype(F32)
    mid = rest.astype(BF16)
    low = (rest - mid.astype(F32)).astype(BF16)
    src = row_of((LANES, chips * LANES))
    dst = lane_of((LANES, chips * LANES))
    head = src % heads
    place = (head // 2) * LANES + RANK + (src // heads) * 6 + (head % 2) * 3
    place = jnp.where(src < 2 * heads, place, -8)
    spread = jnp.zeros((tok, chips * LANES), F32)
    for j, part in enumerate((high, mid, low)):
        pick = jnp.where(dst == place + j, 1.0, 0.0).astype(BF16)
        spread = spread + nn(part, pick)
    for p in range(chips):
        two = slice(p * 2 * HEAD_DIM, (p + 1) * 2 * HEAD_DIM)
        kv = 2 * p // group
        kv_cols = KV_HEADS * HEAD_DIM
        msg_ref[p, :, Q_AT:D_AT] = q_ref[:, two]
        msg_ref[p, :, D_AT:K_AT] = d_ref[:, two]
        msg_ref[p, :, K_AT:V_AT] = kv_ref[:, kv * HEAD_DIM : (kv + 1) * HEAD_DIM]
        msg_ref[p, :, V_AT:X_AT] = kv_ref[:, kv_cols + kv * HEAD_DIM : kv_cols + (kv + 1) * HEAD_DIM]
        block = x + spread[:, p * LANES : (p + 1) * LANES]
        msg_ref[p, :, X_AT:WIDE] = block.astype(BF16)


def attention_kernel(
    at_ref, r_ref, o_ref, pq_ref, pk_ref, pv_ref, out_ref,
    qs, ds, qp, dp_, kp, vp, wa, wb, ps, dss, gq, gk, gv,
):
    chip = at_ref[0]
    core = at_ref[1]
    blocks, tok, _ = r_ref.shape
    rows = blocks * tok
    half = 2 * tok
    groups = rows // half
    group = pk_ref.shape[0] // HEAD_DIM
    heads = pq_ref.shape[0] // HEAD_DIM
    per_kv = heads // group

    def part(ref, at):
        return ref[:, :, at : at + LANES].reshape(rows, LANES)

    lane = lane_of((rows, LANES))
    xl = part(r_ref, X_AT)
    none = jnp.zeros_like(xl)
    kv = (2 * chip) // per_kv
    pk = pk_ref[pl.ds(pl.multiple_of(kv * HEAD_DIM, HEAD_DIM), HEAD_DIM), :]
    pv = pv_ref[pl.ds(pl.multiple_of(kv * HEAD_DIM, HEAD_DIM), HEAD_DIM), :]
    pk = jnp.concatenate([pk, pk], axis=1)
    pv = jnp.concatenate([pv, pv], axis=1)
    first = lane < RANK

    def doubled(a, proj):
        full = nn(a, proj)
        high = full.astype(BF16).astype(F32)
        return jnp.where(first, high, full - high).astype(BF16)

    for h in range(2):
        q = part(r_ref, Q_AT + h * LANES)
        d = part(r_ref, D_AT + h * LANES)
        for ref, val, kind in ((qs, q, 0), (ds, d, 1)):
            start = RANK + kind * 6 + h * 3
            mask = (lane >= start) & (lane < start + 3)
            side = jnp.where(mask, xl, none)
            for g in range(groups):
                ref[g, h * half : (h + 1) * half, :LANES] = val[g * half : (g + 1) * half]
                ref[g, h * half : (h + 1) * half, LANES:] = side[g * half : (g + 1) * half]
        qp[h] = doubled(q, pk)
        dp_[h] = doubled(d, pv)

    ones = jnp.ones((rows, LANES), BF16)
    kp[:, LANES:] = ones
    vp[:, LANES:] = ones
    gq[...] = jnp.zeros_like(gq)
    gk[...] = jnp.zeros_like(gk)
    gv[...] = jnp.zeros_like(gv)
    r_io = row_of((2 * half, half)) % half
    c_io = lane_of((2 * half, half))
    own_seen = c_io <= r_io
    other_seen = (c_io // tok) < (r_io // tok) + core
    fold = SCALE * math.log2(math.e)

    for src, base, seen in ((r_ref, 0, own_seen), (o_ref, K_AT, other_seen)):
        key = part(src, K_AT - base)
        x_key = part(src, X_AT - base)
        kp[:, :LANES] = key
        vp[:, :LANES] = part(src, V_AT - base)
        for h, w in enumerate((wa, wb)):
            at = pl.multiple_of((2 * chip + h) * HEAD_DIM, HEAD_DIM)
            pq = pq_ref[pl.ds(at, HEAD_DIM), :]
            w[:, :LANES] = doubled(key, jnp.concatenate([pq, pq], axis=1))
            w[:, LANES:] = x_key
        for g in range(groups):
            upto = (g + 1) * half
            for n in range(g + 1):
                cols = slice(n * half, (n + 1) * half)
                s = nt(qs[g], kp[cols, :])
                probs = jnp.exp2(s * fold)
                if n == g:
                    probs = jnp.where(seen, probs, 0.0)
                dscores = probs * nt(ds[g], vp[cols, :])
                ps[:, cols] = probs.astype(BF16)
                dss[:, cols] = dscores.astype(BF16)
            acc_v = nn(ps[:, :upto], wa[:upto, LANES:])
            here = slice(g * half, (g + 1) * half)
            for h, w in enumerate((wa, wb)):
                mine = slice(h * half, (h + 1) * half)
                acc = nn(dss[mine, :upto], w[:upto, :])
                high, low = split2(acc)
                vh, vl = split2(acc_v[mine])
                xq = r_ref[2 * g : 2 * g + 2, :, X_AT:WIDE].reshape(half, LANES)
                gq[...] += tn(xq, jnp.concatenate([high[:, :LANES], low[:, :LANES]], axis=1))
                gk[...] += tn(qp[h, here, :], jnp.concatenate([high[:, LANES:], low[:, LANES:]], axis=1))
                gv[...] += tn(dp_[h, here, :], jnp.concatenate([vh, vl], axis=1))

    def quarter(a):
        t = a[:, :LANES] + a[:, LANES:]
        return t

    tq = quarter(gq[:RANK, :])
    out_q = (tq + pltpu.roll(tq, RANK, 1)) * SCALE
    tk = quarter(gk[:RANK, :] + gk[RANK:, :])
    tv = quarter(gv[:RANK, :] + gv[RANK:, :])
    zero = jnp.zeros((RANK, LANES), F32)
    tk = jnp.concatenate([tk, zero], axis=0).T[:RANK] * SCALE
    tv = jnp.concatenate([tv, zero], axis=0).T[:RANK]
    low_lanes = lane_of((RANK, LANES)) < RANK
    top = jnp.where(low_lanes, out_q, pltpu.roll(tk, RANK, 1))
    bottom = jnp.where(
        lane_of((RANK // 2, LANES)) < RANK, tv[: RANK // 2], pltpu.roll(tv, RANK, 1)[RANK // 2 :]
    )
    packed = jnp.concatenate([top, bottom], axis=0).astype(BF16)
    for i in range(out_ref.shape[0]):
        out_ref[i] = packed


def unit_kernel(at_ref, parts_ref, unit_ref, mine_ref, send_ref, flat):
    total = parts_ref[0].astype(F32)
    for i in range(1, parts_ref.shape[0]):
        total = total + parts_ref[i].astype(F32)
    mean = jnp.sum(total * total) / (3.0 * RANK * RANK)
    unit = total / jnp.sqrt(jnp.full((1, LANES), mean, F32) + 1e-6)
    unit_ref[:, :LANES] = unit[:RANK]
    unit_ref[: RANK // 2, LANES:] = unit[RANK:, :RANK]
    unit_ref[RANK // 2 :, LANES:] = unit[RANK:, RANK:]
    flat[...] = jnp.zeros_like(flat)
    flat[: unit.shape[0], :] = unit
    depth = mine_ref.shape[0]
    mine = flat[pl.ds(pl.multiple_of(at_ref[0] * depth, depth), depth), :]
    mine_ref[...] = mine
    send = mine.astype(BF16)
    for i in range(send_ref.shape[0]):
        send_ref[i] = send


def score_kernel(docs_ref, mine_ref, every_ref, out_ref):
    mine = mine_ref[...]
    count = docs_ref.shape[0]
    lane = lane_of((1, LANES))
    res = jnp.zeros((1, LANES), F32)
    for q in range(count):
        other = every_ref[docs_ref[q]].astype(F32)
        res = jnp.where(lane == q, jnp.sum(mine * other), res)
    for i in range(out_ref.shape[0]):
        out_ref[i] = res


def local(
    hidden_in, queries, keys_values, attn_out, out_grad, log_norms, proj_in, proj_q, proj_k, proj_v, query_docs
):
    tok = queries.shape[1]
    heads = log_norms.shape[1]
    chips = heads // 2
    docs = lax.axis_size("dp")
    same_core = [[2 * p + c for p in range(chips)] for c in range(2)]
    index = lax.axis_index("ctx")
    at = jnp.stack([index // 2, index % 2]).astype(jnp.int32)
    params = pltpu.CompilerParams(vmem_limit_bytes=40 * 2**20)

    with jax.named_scope("message"):
        msg = pl.pallas_call(
            message_kernel,
            out_shape=jax.ShapeDtypeStruct((chips, tok, WIDE), BF16),
            in_specs=[VMEM] * 7,
            out_specs=VMEM,
            compiler_params=params,
        )(hidden_in[0], queries[0], keys_values[0], attn_out[0], out_grad[0], log_norms[0], proj_in)
    with jax.named_scope("exchange_heads"):
        got = lax.all_to_all(msg, "ctx", 0, 0, axis_index_groups=same_core, tiled=True)
    with jax.named_scope("swap_cores"):
        other = lax.ppermute(got[:, :, K_AT:], "ctx", [(i, i ^ 1) for i in range(2 * chips)])
    rows = chips * tok
    half = 2 * tok
    groups = rows // half
    with jax.named_scope("attention"):
        partial = pl.pallas_call(
            attention_kernel,
            out_shape=jax.ShapeDtypeStruct((2 * chips, 3 * RANK // 2, LANES), BF16),
            in_specs=[SMEM] + [VMEM] * 5,
            out_specs=VMEM,
            scratch_shapes=[
                pltpu.VMEM((groups, 2 * half, 2 * LANES), BF16),
                pltpu.VMEM((groups, 2 * half, 2 * LANES), BF16),
                pltpu.VMEM((2, rows, LANES), BF16),
                pltpu.VMEM((2, rows, LANES), BF16),
                pltpu.VMEM((rows, 2 * LANES), BF16),
                pltpu.VMEM((rows, 2 * LANES), BF16),
                pltpu.VMEM((rows, 2 * LANES), BF16),
                pltpu.VMEM((rows, 2 * LANES), BF16),
                pltpu.VMEM((2 * half, rows), BF16),
                pltpu.VMEM((2 * half, rows), BF16),
                pltpu.VMEM((LANES, 2 * LANES), F32),
                pltpu.VMEM((LANES, 2 * LANES), F32),
                pltpu.VMEM((LANES, 2 * LANES), F32),
            ],
            compiler_params=params,
        )(at, got, other, proj_q, proj_k, proj_v)
    with jax.named_scope("sum_parts"):
        parts = lax.all_to_all(partial, "ctx", 0, 0, tiled=True)
    with jax.named_scope("unit"):
        unit, mine, send = pl.pallas_call(
            unit_kernel,
            out_shape=(
                jax.ShapeDtypeStruct((RANK, 3 * RANK), F32),
                jax.ShapeDtypeStruct((16, LANES), F32),
                jax.ShapeDtypeStruct((docs, 16, LANES), BF16),
            ),
            in_specs=[SMEM, VMEM],
            out_specs=(VMEM, VMEM, VMEM),
            scratch_shapes=[pltpu.VMEM((16 * chips, LANES), F32)],
        )(at, parts)
    with jax.named_scope("exchange_documents"):
        every = lax.all_to_all(send, "dp", 0, 0, tiled=True)
    with jax.named_scope("score"):
        terms = pl.pallas_call(
            score_kernel,
            out_shape=jax.ShapeDtypeStruct((chips, 1, LANES), F32),
            in_specs=[SMEM, VMEM, VMEM],
            out_specs=VMEM,
        )(query_docs, mine, every)
    with jax.named_scope("sum_scores"):
        terms = lax.all_to_all(terms, "ctx", 0, 0, axis_index_groups=same_core, tiled=True)
    scores = jnp.sum(terms[:, :, : query_docs.shape[0]], axis=0) / (3.0 * RANK * RANK)
    return (unit.reshape(1, -1), scores)


def solution(mesh):
    in_specs = (
        P("dp", "ctx", None),
        P("dp", "ctx", None),
        P("dp", "ctx", None),
        P("dp", "ctx", None),
        P("dp", "ctx", None),
        P("dp", None, "ctx"),
        P(),
        P(),
        P(),
        P(),
        P(),
    )
    out_specs = (P("dp", None), P("dp", None))
    return jax.shard_map(local, mesh=mesh, in_specs=in_specs, out_specs=out_specs, check_vma=False)
```

```python
import functools
import math

import jax
import jax.numpy as jnp
from jax import lax
from jax.experimental import pallas as pl
from jax.experimental.pallas import tpu as pltpu
from jax.sharding import PartitionSpec as P

KV_HEADS = 4
HEAD_DIM = 128
RANK = 64
LANES = 128
SCALE = HEAD_DIM ** (-0.5)
F32 = jnp.float32
BF16 = jnp.bfloat16
VMEM = pl.BlockSpec(memory_space=pltpu.VMEM)
SMEM = pl.BlockSpec(memory_space=pltpu.SMEM)

HBM = pl.BlockSpec(memory_space=pltpu.HBM)

Q_AT, D_AT, K_AT, V_AT, X_AT, WIDE = 0, 256, 512, 640, 768, 896


def nt(a, b):
    return lax.dot_general(a, b, (((1,), (1,)), ((), ())), preferred_element_type=F32)


def tn(a, b):
    return lax.dot_general(a, b, (((0,), (0,)), ((), ())), preferred_element_type=F32)


def nn(a, b):
    return jnp.dot(a, b, preferred_element_type=F32)


def split2(a):
    high = a.astype(BF16)
    return high, (a - high.astype(F32)).astype(BF16)


def lane_of(shape):
    return lax.broadcasted_iota(jnp.int32, shape, len(shape) - 1)


def row_of(shape):
    return lax.broadcasted_iota(jnp.int32, shape, len(shape) - 2)


def start_all(pairs, sems):
    copies = [pltpu.make_async_copy(src, dst, sems.at[i]) for i, (src, dst) in enumerate(pairs)]
    for copy in copies:
        copy.start()
    return copies


def row_parts(src, dst, parts):
    rows = src.shape[0] // parts
    return [(src.at[pl.ds(i * rows, rows)], dst.at[pl.ds(i * rows, rows)]) for i in range(parts)]


def message_kernel(
    h_hbm, q_hbm, kv_hbm, o_hbm, d_hbm, lse_hbm, pin_hbm, msg_ref, h_ref, kv_ref, o_ref, d_ref, lse_ref, pin_ref, sems
):
    tok = kv_ref.shape[0]
    heads = lse_ref.shape[0]
    chips = heads // 2
    group = heads // KV_HEADS
    two = 2 * HEAD_DIM
    parts = 2
    todo = [(lse_hbm, lse_ref)] + row_parts(d_hbm, d_ref, parts) + row_parts(o_hbm, o_ref, parts)
    deltas = len(todo)
    todo += [(pin_hbm, pin_ref)] + row_parts(h_hbm, h_ref, parts) + row_parts(kv_hbm, kv_ref, parts)
    inputs = len(todo)
    todo += [(q_hbm.at[:, pl.ds(p * two, two)], msg_ref.at[p, :, pl.ds(Q_AT, two)]) for p in range(chips)]
    copies = start_all(todo, sems)
    src = row_of((LANES, chips * LANES))
    dst = lane_of((LANES, chips * LANES))
    head = src % heads
    place = (head // 2) * LANES + RANK + (src // heads) * 6 + (head % 2) * 3
    place = jnp.where(src < 2 * heads, place, -8)
    picks = [jnp.where(dst == place + j, 1.0, 0.0).astype(BF16) for j in range(3)]
    for copy in copies[:deltas]:
        copy.wait()
    lse = jnp.concatenate([lse_ref[...], jnp.zeros((LANES - heads, tok), F32)], axis=0)
    terms = lse.T * (-1.0 / SCALE)
    lane = lane_of((tok, LANES))
    for h in range(heads):
        cols = slice(h * HEAD_DIM, (h + 1) * HEAD_DIM)
        prod = d_ref[:, cols].astype(F32) * o_ref[:, cols].astype(F32)
        delta = jnp.sum(prod, axis=1, keepdims=True)
        terms = jnp.where(lane == heads + h, -delta, terms)
    high = terms.astype(BF16)
    rest = terms - high.astype(F32)
    mid = rest.astype(BF16)
    low = (rest - mid.astype(F32)).astype(BF16)
    spread = nn(high, picks[0]) + nn(mid, picks[1]) + nn(low, picks[2])
    for p in range(chips):
        msg_ref[p, :, D_AT:K_AT] = d_ref[:, p * two : (p + 1) * two]
    for copy in copies[deltas:inputs]:
        copy.wait()
    x = nt(h_ref[...], pin_ref[...])
    x = jnp.concatenate([x, jnp.zeros((tok, LANES - RANK), F32)], axis=1)
    kv_cols = KV_HEADS * HEAD_DIM
    for p in range(chips):
        kv = 2 * p // group
        msg_ref[p, :, K_AT:V_AT] = kv_ref[:, kv * HEAD_DIM : (kv + 1) * HEAD_DIM]
        msg_ref[p, :, V_AT:X_AT] = kv_ref[:, kv_cols + kv * HEAD_DIM : kv_cols + (kv + 1) * HEAD_DIM]
        block = x + spread[:, p * LANES : (p + 1) * LANES]
        msg_ref[p, :, X_AT:] = block.astype(BF16)
    for copy in copies[inputs:]:
        copy.wait()


def message_call(hidden_in, queries, keys_values, attn_out, out_grad, log_norms, proj_in_t):
    tok = queries.shape[0]
    chips = log_norms.shape[0] // 2
    return pl.pallas_call(
        message_kernel,
        out_shape=jax.ShapeDtypeStruct((chips, tok, WIDE), BF16),
        in_specs=[HBM] * 7,
        out_specs=VMEM,
        scratch_shapes=[
            pltpu.VMEM(a.shape, a.dtype)
            for a in (hidden_in, keys_values, attn_out, out_grad, log_norms, proj_in_t)
        ]
        + [pltpu.SemaphoreType.DMA((2 + 4 * 2 + chips,))],
        compiler_params=pltpu.CompilerParams(vmem_limit_bytes=60 * 2**20),
    )(hidden_in, queries, keys_values, attn_out, out_grad, log_norms, proj_in_t)


def attention_kernel(
    at_ref, r_ref, o_ref, pq_ref, pk_ref, pv_ref, out_ref, qs, ds, qp, dp_, kt, vt, w, xk, ps, dss, rq, rk, rv,
):
    chip = at_ref[0]
    core = at_ref[1]
    blocks, tok, _ = r_ref.shape
    rows = blocks * tok
    half = 2 * tok
    groups = rows // half
    group = pk_ref.shape[1] // HEAD_DIM
    heads = pq_ref.shape[1] // HEAD_DIM
    per_kv = heads // group

    def part(ref, at):
        return ref[:, :, at : at + LANES].reshape(rows, LANES)

    lane = lane_of((rows, LANES))
    xl = part(r_ref, X_AT)
    none = jnp.zeros_like(xl)
    kv = (2 * chip) // per_kv
    kv_at = pl.ds(pl.multiple_of(kv * HEAD_DIM, HEAD_DIM), HEAD_DIM)
    pk = jnp.concatenate([pk_ref[:, kv_at]] * 2, axis=0)
    pv = jnp.concatenate([pv_ref[:, kv_at]] * 2, axis=0)
    first = lane < RANK

    def doubled(a, proj):
        full = nt(a, proj)
        high = full.astype(BF16).astype(F32)
        return jnp.where(first, high, full - high).astype(BF16)

    for h in range(2):
        q = part(r_ref, Q_AT + h * LANES)
        d = part(r_ref, D_AT + h * LANES)
        for ref, val, kind in ((qs, q, 0), (ds, d, 1)):
            start = RANK + kind * 6 + h * 3
            mask = (lane >= start) & (lane < start + 3)
            side = jnp.where(mask, xl, none)
            for g in range(groups):
                ref[g, h * half : (h + 1) * half, :LANES] = val[g * half : (g + 1) * half]
                ref[g, h * half : (h + 1) * half, LANES:] = side[g * half : (g + 1) * half]
        qp[h * rows : (h + 1) * rows] = doubled(q, pk)
        dp_[h * rows : (h + 1) * rows] = doubled(d, pv)

    kt[:, LANES:, :] = jnp.ones((2, LANES, rows), BF16)
    vt[:, LANES:, :] = jnp.ones((2, LANES, rows), BF16)
    for i, (src, base) in enumerate(((r_ref, 0), (o_ref, K_AT))):
        key = part(src, K_AT - base)
        kt[i, :LANES, :] = key.T
        vt[i, :LANES, :] = part(src, V_AT - base).T
        xk[i] = part(src, X_AT - base)
        for h in range(2):
            at = pl.multiple_of((2 * chip + h) * HEAD_DIM, HEAD_DIM)
            pq = pq_ref[:, pl.ds(at, HEAD_DIM)]
            w[h, i, :, :LANES] = doubled(key, jnp.concatenate([pq, pq], axis=0))
            w[h, i, :, LANES:] = xk[i]

    RB = 256
    fold = SCALE * math.log2(math.e)
    r_io = row_of((RB, half))
    c_io = lane_of((RB, half))
    for g in range(groups):
        upto = (g + 1) * half
        for i in range(2):
            for n in range(g + 1):
                cols = slice(n * half, (n + 1) * half)
                for r0 in range(0, 2 * half, RB):
                    rr = slice(r0, r0 + RB)
                    s = nn(qs[g, rr], kt[i, :, cols])
                    probs = jnp.exp2(s * fold)
                    if n == g:
                        ri = (r_io + r0) % half
                        if i == 0:
                            seen = c_io <= ri
                        else:
                            seen = (c_io // tok) < (ri // tok) + core
                        probs = jnp.where(seen, probs, 0.0)
                    dscores = probs * nn(ds[g, rr], vt[i, :, cols])
                    ps[i, rr, cols] = probs.astype(BF16)
                    dss[i, rr, cols] = dscores.astype(BF16)
        acc_v = nn(ps[0, :, :upto], xk[0, :upto]) + nn(ps[1, :, :upto], xk[1, :upto])
        vh, vl = split2(acc_v)
        sum_q = None
        for h in range(2):
            mine = slice(h * half, (h + 1) * half)
            to = slice(h * rows + g * half, h * rows + (g + 1) * half)
            acc = nn(dss[0, mine, :upto], w[h, 0, :upto]) + nn(dss[1, mine, :upto], w[h, 1, :upto])
            rv[to, :LANES] = vh[mine]
            rv[to, LANES:] = vl[mine]
            high, low = split2(acc[:, LANES:])
            rk[to, :LANES] = high
            rk[to, LANES:] = low
            sum_q = acc[:, :LANES] if h == 0 else sum_q + acc[:, :LANES]
        high, low = split2(sum_q)
        rq[g * half : (g + 1) * half, :LANES] = high
        rq[g * half : (g + 1) * half, LANES:] = low
    gq = tn(xl, rq[...])
    gk = tn(qp[...], rk[...])
    gv = tn(dp_[...], rv[...])

    def halves(a):
        return a[:, :LANES] + a[:, LANES:]

    tq = halves(gq[:RANK, :])
    out_q = (tq + pltpu.roll(tq, RANK, 1)) * SCALE
    tk = halves(gk[:RANK, :] + gk[RANK:, :])
    tv = halves(gv[:RANK, :] + gv[RANK:, :])
    zero = jnp.zeros((RANK, LANES), F32)
    tk = jnp.concatenate([tk, zero], axis=0).T[:RANK] * SCALE
    tv = jnp.concatenate([tv, zero], axis=0).T[:RANK]
    low_lanes = lane_of((RANK, LANES)) < RANK
    top = jnp.where(low_lanes, out_q, pltpu.roll(tk, RANK, 1))
    bottom = jnp.where(
        lane_of((RANK // 2, LANES)) < RANK, tv[: RANK // 2], pltpu.roll(tv, RANK, 1)[RANK // 2 :]
    )
    packed = jnp.concatenate([top, bottom], axis=0).astype(BF16)
    for i in range(out_ref.shape[0]):
        out_ref[i] = packed


def attention_call(at, got, other, proj_q, proj_k, proj_v):
    chips, tok, _ = got.shape
    rows = chips * tok
    half = 2 * tok
    groups = rows // half
    return pl.pallas_call(
        attention_kernel,
        out_shape=jax.ShapeDtypeStruct((2 * chips, 3 * RANK // 2, LANES), BF16),
        in_specs=[SMEM] + [VMEM] * 5,
        out_specs=VMEM,
        scratch_shapes=[
            pltpu.VMEM((groups, 2 * half, 2 * LANES), BF16),
            pltpu.VMEM((groups, 2 * half, 2 * LANES), BF16),
            pltpu.VMEM((2 * rows, LANES), BF16),
            pltpu.VMEM((2 * rows, LANES), BF16),
            pltpu.VMEM((2, 2 * LANES, rows), BF16),
            pltpu.VMEM((2, 2 * LANES, rows), BF16),
            pltpu.VMEM((2, 2, rows, 2 * LANES), BF16),
            pltpu.VMEM((2, rows, LANES), BF16),
            pltpu.VMEM((2, 2 * half, rows), BF16),
            pltpu.VMEM((2, 2 * half, rows), BF16),
            pltpu.VMEM((rows, 2 * LANES), BF16),
            pltpu.VMEM((2 * rows, 2 * LANES), BF16),
            pltpu.VMEM((2 * rows, 2 * LANES), BF16),
        ],
        compiler_params=pltpu.CompilerParams(vmem_limit_bytes=40 * 2**20),
    )(at, got, other, proj_q, proj_k, proj_v)


def unit_kernel(at_ref, parts_ref, unit_ref, mine_ref, send_ref, flat):
    total = parts_ref[0].astype(F32)
    for i in range(1, parts_ref.shape[0]):
        total = total + parts_ref[i].astype(F32)
    mean = jnp.sum(jnp.sum(total * total, axis=0, keepdims=True), axis=1, keepdims=True) / (3.0 * RANK * RANK)
    unit = total / jnp.sqrt(mean + 1e-6)
    unit_ref[:, :LANES] = unit[:RANK]
    unit_ref[: RANK // 2, LANES:] = unit[RANK:, :RANK]
    unit_ref[RANK // 2 :, LANES:] = unit[RANK:, RANK:]
    flat[: unit.shape[0], :] = unit
    flat[unit.shape[0] :, :] = jnp.zeros((flat.shape[0] - unit.shape[0], LANES), F32)
    depth = mine_ref.shape[0]
    mine = flat[pl.ds(pl.multiple_of(at_ref[0] * depth, depth), depth), :]
    mine_ref[...] = mine
    send = mine.astype(BF16)
    for i in range(send_ref.shape[0]):
        send_ref[i] = send


def score_kernel(docs_ref, mine_ref, every_ref, out_ref):
    mine = mine_ref[...]
    terms = []
    for q in range(docs_ref.shape[0]):
        other = every_ref[docs_ref[q]].astype(F32)
        terms.append(jnp.sum(mine * other, axis=0, keepdims=True))
    terms = jnp.concatenate(terms, axis=0)
    for i in range(out_ref.shape[0]):
        out_ref[i] = terms


def local(
    hidden_in, queries, keys_values, attn_out, out_grad, log_norms, proj_in, proj_q, proj_k, proj_v, query_docs
):
    tok = queries.shape[1]
    heads = log_norms.shape[1]
    chips = heads // 2
    docs = lax.axis_size("dp")
    count = query_docs.shape[0]
    same_core = [[2 * p + c for p in range(chips)] for c in range(2)]
    index = lax.axis_index("ctx")
    at = jnp.stack([lax.shift_right_logical(index, 1), index & 1])

    with jax.named_scope("message"):
        msg = message_call(
            hidden_in[0], queries[0], keys_values[0], attn_out[0], out_grad[0], log_norms[0], proj_in.T
        )
    with jax.named_scope("exchange_heads"):
        got = lax.all_to_all(msg, "ctx", 0, 0, axis_index_groups=same_core, tiled=True)
    with jax.named_scope("swap_cores"):
        other = lax.ppermute(got[:, :, K_AT:], "ctx", [(i, i ^ 1) for i in range(2 * chips)])
    with jax.named_scope("attention"):
        partial = attention_call(at, got, other, proj_q.T, proj_k.T, proj_v.T)
    with jax.named_scope("sum_parts"):
        parts = lax.all_to_all(partial, "ctx", 0, 0, tiled=True)
    with jax.named_scope("unit"):
        unit, mine, send = pl.pallas_call(
            unit_kernel,
            out_shape=(
                jax.ShapeDtypeStruct((RANK, 3 * RANK), F32),
                jax.ShapeDtypeStruct((16, LANES), F32),
                jax.ShapeDtypeStruct((docs, 16, LANES), BF16),
            ),
            in_specs=[SMEM, VMEM],
            out_specs=(VMEM, VMEM, VMEM),
            scratch_shapes=[pltpu.VMEM((16 * chips, LANES), F32)],
            compiler_params=pltpu.CompilerParams(vmem_limit_bytes=8 * 2**20),
        )(at, parts)
    with jax.named_scope("exchange_documents"):
        every = lax.all_to_all(send, "dp", 0, 0, tiled=True)
    with jax.named_scope("score"):
        terms = pl.pallas_call(
            score_kernel,
            out_shape=jax.ShapeDtypeStruct((chips, count, LANES), F32),
            in_specs=[SMEM, VMEM, VMEM],
            out_specs=VMEM,
            compiler_params=pltpu.CompilerParams(vmem_limit_bytes=8 * 2**20),
        )(query_docs, mine, every)
    with jax.named_scope("sum_scores"):
        terms = lax.all_to_all(terms, "ctx", 0, 0, axis_index_groups=same_core, tiled=True)
    scores = jnp.sum(terms, axis=(0, 2))[None] / (3.0 * RANK * RANK)
    return (unit.reshape(1, -1), scores)


def solution(mesh):
    in_specs = (
        P("dp", "ctx", None),
        P("dp", "ctx", None),
        P("dp", "ctx", None),
        P("dp", "ctx", None),
        P("dp", "ctx", None),
        P("dp", None, "ctx"),
        P(),
        P(),
        P(),
        P(),
        P(),
    )
    out_specs = (P("dp", None), P("dp", None))
    return jax.shard_map(local, mesh=mesh, in_specs=in_specs, out_specs=out_specs, check_vma=False)
```

```python
import functools
import math

import jax
import jax.numpy as jnp
from jax import lax
from jax.experimental import pallas as pl
from jax.experimental.pallas import tpu as pltpu
from jax.sharding import PartitionSpec as P

KV_HEADS = 4
HEAD_DIM = 128
RANK = 64
LANES = 128
SCALE = HEAD_DIM ** (-0.5)
F32 = jnp.float32
BF16 = jnp.bfloat16
VMEM = pl.BlockSpec(memory_space=pltpu.VMEM)
SMEM = pl.BlockSpec(memory_space=pltpu.SMEM)

HBM = pl.BlockSpec(memory_space=pltpu.HBM)

Q_AT, D_AT, V_AT, K_AT, X_AT, WIDE = 0, 256, 512, 640, 768, 896


def nt(a, b):
    return lax.dot_general(a, b, (((1,), (1,)), ((), ())), preferred_element_type=F32)


def tn(a, b):
    return lax.dot_general(a, b, (((0,), (0,)), ((), ())), preferred_element_type=F32)


def nn(a, b):
    return jnp.dot(a, b, preferred_element_type=F32)


def split2(a):
    high = a.astype(BF16)
    return high, (a - high.astype(F32)).astype(BF16)


def lane_of(shape):
    return lax.broadcasted_iota(jnp.int32, shape, len(shape) - 1)


def row_of(shape):
    return lax.broadcasted_iota(jnp.int32, shape, len(shape) - 2)


def place():
    index = lax.axis_index("ctx")
    return lax.div(index, 2), lax.rem(index, 2)


def start_all(pairs, sems):
    copies = [pltpu.make_async_copy(src, dst, sems.at[i]) for i, (src, dst) in enumerate(pairs)]
    for copy in copies:
        copy.start()
    return copies


def row_parts(src, dst, parts):
    rows = src.shape[0] // parts
    return [(src.at[pl.ds(i * rows, rows)], dst.at[pl.ds(i * rows, rows)]) for i in range(parts)]


def message_kernel(
    h_hbm, q_hbm, kv_hbm, o_hbm, d_hbm, lse_hbm, pin_hbm, pq_hbm, pk_hbm, pv_hbm, msg_ref, proj_ref,
    h_ref, kv_ref, o_ref, d_ref, lse_ref, pin_ref, sems,
):
    tok = kv_ref.shape[0]
    heads = lse_ref.shape[0]
    chips = heads // 2
    group = heads // KV_HEADS
    two = 2 * HEAD_DIM
    parts = 2
    chip, _ = place()
    kv_at = head_at(lax.div(2 * chip, group))
    pairs = pl.ds(pl.multiple_of(chip * two, two), two)
    todo = [(pq_hbm.at[:, pairs], proj_ref.at[:, pl.ds(0, two)])]
    todo += [(pk_hbm.at[:, kv_at], proj_ref.at[:, pl.ds(two, HEAD_DIM)])]
    todo += [(pv_hbm.at[:, kv_at], proj_ref.at[:, pl.ds(two + HEAD_DIM, HEAD_DIM)])]
    todo += [(lse_hbm, lse_ref)] + row_parts(d_hbm, d_ref, parts) + row_parts(o_hbm, o_ref, parts)
    deltas = len(todo)
    todo += [(pin_hbm, pin_ref)] + row_parts(h_hbm, h_ref, parts) + row_parts(kv_hbm, kv_ref, parts)
    inputs = len(todo)
    todo += [(q_hbm.at[:, pl.ds(p * two, two)], msg_ref.at[p, :, pl.ds(Q_AT, two)]) for p in range(chips)]
    copies = start_all(todo, sems)
    src = row_of((LANES, chips * LANES))
    dst = lane_of((LANES, chips * LANES))
    head = src % heads
    to = (head // 2) * LANES + RANK + (src // heads) * 6 + (head % 2) * 3
    to = jnp.where(src < 2 * heads, to, -8)
    picks = [jnp.where(dst == to + j, 1.0, 0.0).astype(BF16) for j in range(3)]
    for copy in copies[:deltas]:
        copy.wait()
    lse = jnp.concatenate([lse_ref[...], jnp.zeros((LANES - heads, tok), F32)], axis=0)
    terms = lse.T * (-1.0 / SCALE)
    lane = lane_of((tok, LANES))
    for h in range(heads):
        cols = slice(h * HEAD_DIM, (h + 1) * HEAD_DIM)
        prod = d_ref[:, cols].astype(F32) * o_ref[:, cols].astype(F32)
        delta = jnp.sum(prod, axis=1, keepdims=True)
        terms = jnp.where(lane == heads + h, -delta, terms)
    high = terms.astype(BF16)
    rest = terms - high.astype(F32)
    mid = rest.astype(BF16)
    low = (rest - mid.astype(F32)).astype(BF16)
    spread = nn(high, picks[0]) + nn(mid, picks[1]) + nn(low, picks[2])
    for p in range(chips):
        msg_ref[p, :, D_AT:V_AT] = d_ref[:, p * two : (p + 1) * two]
    for copy in copies[deltas:inputs]:
        copy.wait()
    x = nt(h_ref[...], pin_ref[...])
    x = jnp.concatenate([x, jnp.zeros((tok, LANES - RANK), F32)], axis=1)
    kv_cols = KV_HEADS * HEAD_DIM
    for p in range(chips):
        kv = 2 * p // group
        msg_ref[p, :, V_AT:K_AT] = kv_ref[:, kv_cols + kv * HEAD_DIM : kv_cols + (kv + 1) * HEAD_DIM]
        msg_ref[p, :, K_AT:X_AT] = kv_ref[:, kv * HEAD_DIM : (kv + 1) * HEAD_DIM]
        block = x + spread[:, p * LANES : (p + 1) * LANES]
        msg_ref[p, :, X_AT:] = block.astype(BF16)
    for copy in copies[inputs:]:
        copy.wait()


def message_call(hidden_in, queries, keys_values, attn_out, out_grad, log_norms, proj_in_t, *proj_t):
    tok = queries.shape[0]
    chips = log_norms.shape[0] // 2
    return pl.pallas_call(
        message_kernel,
        out_shape=(
            jax.ShapeDtypeStruct((chips, tok, WIDE), BF16),
            jax.ShapeDtypeStruct((RANK, 4 * HEAD_DIM), BF16),
        ),
        in_specs=[HBM] * 10,
        out_specs=(VMEM, VMEM),
        scratch_shapes=[
            pltpu.VMEM(a.shape, a.dtype)
            for a in (hidden_in, keys_values, attn_out, out_grad, log_norms, proj_in_t)
        ]
        + [pltpu.SemaphoreType.DMA((13 + chips,))],
        compiler_params=pltpu.CompilerParams(vmem_limit_bytes=60 * 2**20),
    )(hidden_in, queries, keys_values, attn_out, out_grad, log_norms, proj_in_t, *proj_t)


def part(ref, at):
    return ref[:, :, at : at + LANES].reshape(ref.shape[0] * ref.shape[1], LANES)


def head_at(index):
    return pl.ds(pl.multiple_of(index * HEAD_DIM, HEAD_DIM), HEAD_DIM)


def load_keys(ref, base, kt, vt):
    rows = ref.shape[0] * ref.shape[1]
    for to, at in ((kt, K_AT), (vt, V_AT)):
        to[:LANES, :] = part(ref, at - base).T
        to[LANES:, :] = jnp.ones((LANES, rows), BF16)


def group_terms(g, tok, base, seen_of, qs, ds, keys_ref, kt, vt, ps, dss):
    half = 2 * tok
    upto = (g + 1) * half
    fold = SCALE * math.log2(math.e)
    for n in range(g + 1):
        cols = slice(n * half, (n + 1) * half)
        for h in range(2):
            rr = slice(h * half, (h + 1) * half)
            s = nn(qs[g, rr], kt[:, cols])
            probs = jnp.exp2(s * fold)
            if n == g:
                probs = jnp.where(seen_of(row_of((half, half)), lane_of((half, half))), probs, 0.0)
            dscores = probs * nn(ds[g, rr], vt[:, cols])
            ps[rr, cols] = probs.astype(BF16)
            dss[rr, cols] = dscores.astype(BF16)
    keys = keys_ref[: 2 * (g + 1), :, K_AT - base :].reshape(upto, 2 * LANES)
    return nn(ps[:, :upto], keys[:, LANES:]), nn(dss[:, :upto], keys)


def own_kernel(r_ref, qs, ds, acc, acc_v, kt, vt, ps, dss):
    blocks, tok, _ = r_ref.shape
    rows = blocks * tok
    half = 2 * tok
    groups = rows // half
    lane = lane_of((rows, LANES))
    xl = part(r_ref, X_AT)
    none = jnp.zeros_like(xl)
    load_keys(r_ref, 0, kt, vt)
    for h in range(2):
        for ref, at, kind in ((qs, Q_AT, 0), (ds, D_AT, 1)):
            val = part(r_ref, at + h * LANES)
            start = RANK + kind * 6 + h * 3
            side = jnp.where((lane >= start) & (lane < start + 3), xl, none)
            for g in range(groups):
                ref[g, h * half : (h + 1) * half, :LANES] = val[g * half : (g + 1) * half]
                ref[g, h * half : (h + 1) * half, LANES:] = side[g * half : (g + 1) * half]
    for g in range(groups):
        to = slice(2 * g * half, 2 * (g + 1) * half)
        acc_v[to], acc[to] = group_terms(g, tok, 0, lambda r, c: c <= r, qs, ds, r_ref, kt, vt, ps, dss)


def other_kernel(r_ref, o_ref, proj_ref, qs, ds, acc, acc_v, out_ref, kt, vt, ps, dss, rq, rk, rv):
    _, core = place()
    blocks, tok, _ = r_ref.shape
    rows = blocks * tok
    half = 2 * tok
    groups = rows // half
    load_keys(o_ref, V_AT, kt, vt)

    def seen_of(r, c):
        return (c // tok) < (r // tok) + core

    for g in range(groups):
        to = slice(2 * g * half, 2 * (g + 1) * half)
        for_v, for_qk = group_terms(g, tok, V_AT, seen_of, qs, ds, o_ref, kt, vt, ps, dss)
        for_v, for_qk = for_v + acc_v[to], for_qk + acc[to]
        for ref, val in ((rv, for_v), (rk, for_qk[:, LANES:]), (rq, for_qk[:, :LANES])):
            high, low = split2(val)
            for h in range(2):
                mine = slice(h * half, (h + 1) * half)
                at = slice(h * rows + g * half, h * rows + (g + 1) * half)
                ref[at, :LANES] = high[mine]
                ref[at, LANES:] = low[mine]

    def halves(a):
        return a[:, :LANES] + a[:, LANES:]

    def exact(a, b, product):
        high, low = split2(a)
        return product(high, b) + product(low, b)

    xl = part(r_ref, X_AT)
    zero = jnp.zeros((RANK, LANES), F32)
    out_q = zero
    mk = jnp.zeros((LANES, LANES), F32)
    mv = jnp.zeros((LANES, LANES), F32)
    for h in range(2):
        at = slice(h * rows, (h + 1) * rows)
        mq = halves(tn(xl, rq[at])[:RANK])
        pq = jnp.concatenate([proj_ref[:, h * HEAD_DIM : (h + 1) * HEAD_DIM], zero.astype(BF16)], axis=0)
        out_q = out_q + exact(mq, pq, nt)
        mk = mk + halves(tn(part(r_ref, Q_AT + h * LANES), rk[at]))
        mv = mv + halves(tn(part(r_ref, D_AT + h * LANES), rv[at]))
    mk_high, mk_low = split2(mk)
    mv_high, mv_low = split2(mv)
    pk = proj_ref[:, 2 * HEAD_DIM : 3 * HEAD_DIM]
    pv = proj_ref[:, 3 * HEAD_DIM :]
    tk = nn(pk, mk_high) + nn(pk, mk_low)
    tv = nn(pv, mv_high) + nn(pv, mv_low)
    tk = jnp.concatenate([tk, zero], axis=0).T[:RANK] * SCALE
    tv = jnp.concatenate([tv, zero], axis=0).T[:RANK]
    low_lanes = lane_of((RANK, LANES)) < RANK
    top = jnp.where(low_lanes, out_q * SCALE, pltpu.roll(tk, RANK, 1))
    bottom = jnp.where(low_lanes[: RANK // 2], tv[: RANK // 2], pltpu.roll(tv, RANK, 1)[RANK // 2 :])
    packed = jnp.concatenate([top, bottom], axis=0).astype(BF16)
    for i in range(out_ref.shape[0]):
        out_ref[i] = packed


def keys_kernel(r_ref, out_ref):
    out_ref[...] = r_ref[:, :, V_AT:]


def keys_call(got):
    chips, tok, _ = got.shape
    return pl.pallas_call(
        keys_kernel,
        out_shape=jax.ShapeDtypeStruct((chips, tok, WIDE - V_AT), BF16),
        in_specs=[VMEM],
        out_specs=VMEM,
        compiler_params=pltpu.CompilerParams(vmem_limit_bytes=8 * 2**20),
    )(got)


def attention_scratch(rows, half):
    return [
        pltpu.VMEM((2 * LANES, rows), BF16),
        pltpu.VMEM((2 * LANES, rows), BF16),
        pltpu.VMEM((2 * half, rows), BF16),
        pltpu.VMEM((2 * half, rows), BF16),
    ]


def own_call(got):
    chips, tok, _ = got.shape
    rows = chips * tok
    half = 2 * tok
    groups = rows // half
    return pl.pallas_call(
        own_kernel,
        out_shape=(
            jax.ShapeDtypeStruct((groups, 2 * half, 2 * LANES), BF16),
            jax.ShapeDtypeStruct((groups, 2 * half, 2 * LANES), BF16),
            jax.ShapeDtypeStruct((2 * rows, 2 * LANES), F32),
            jax.ShapeDtypeStruct((2 * rows, LANES), F32),
        ),
        in_specs=[VMEM],
        out_specs=(VMEM,) * 4,
        scratch_shapes=attention_scratch(rows, half),
        compiler_params=pltpu.CompilerParams(vmem_limit_bytes=24 * 2**20),
        cost_estimate=pl.CostEstimate(
            flops=2 * 4 * 2 * rows * rows * 2 * LANES, bytes_accessed=8 * 2**20, transcendentals=rows * rows
        ),
    )(got)


def other_call(got, other, proj, saved):
    chips, tok, _ = got.shape
    rows = chips * tok
    half = 2 * tok
    return pl.pallas_call(
        other_kernel,
        out_shape=jax.ShapeDtypeStruct((2 * chips, 3 * RANK // 2, LANES), BF16),
        in_specs=[VMEM] * 7,
        out_specs=VMEM,
        scratch_shapes=attention_scratch(rows, half) + [pltpu.VMEM((2 * rows, 2 * LANES), BF16)] * 3,
        compiler_params=pltpu.CompilerParams(vmem_limit_bytes=24 * 2**20),
    )(got, other, proj, *saved)


def attention_call(got, other, proj):
    return other_call(got, other, proj, own_call(got))


def unit_kernel(parts_ref, unit_ref, mine_ref, send_ref, flat):
    total = parts_ref[0].astype(F32)
    for i in range(1, parts_ref.shape[0]):
        total = total + parts_ref[i].astype(F32)
    mean = jnp.sum(jnp.sum(total * total, axis=0, keepdims=True), axis=1, keepdims=True) / (3.0 * RANK * RANK)
    unit = total / jnp.sqrt(mean + 1e-6)
    unit_ref[:, :LANES] = unit[:RANK]
    unit_ref[: RANK // 2, LANES:] = unit[RANK:, :RANK]
    unit_ref[RANK // 2 :, LANES:] = unit[RANK:, RANK:]
    flat[: unit.shape[0], :] = unit
    flat[unit.shape[0] :, :] = jnp.zeros((flat.shape[0] - unit.shape[0], LANES), F32)
    depth = mine_ref.shape[0]
    chip, _ = place()
    mine = flat[pl.ds(pl.multiple_of(chip * depth, depth), depth), :]
    mine_ref[...] = mine
    send = mine.astype(BF16)
    for i in range(send_ref.shape[0]):
        send_ref[i] = send


def split3(a):
    high, rest = split2(a)
    rest = a - high.astype(F32)
    mid, low = split2(rest)
    return high, mid, low


def score_kernel(docs_ref, mine_ref, every_ref, out_ref):
    mine = mine_ref[...]
    docs = every_ref.shape[0]
    terms = [jnp.sum(mine * every_ref[e].astype(F32), axis=0, keepdims=True) for e in range(docs)]
    terms = jnp.concatenate(terms, axis=0)
    ones = jnp.ones((8, LANES), BF16)
    sums = sum(nt(ones, t) for t in split3(terms))
    asked = docs_ref[...]
    picks = jnp.where(row_of((docs, asked.shape[1])) == asked, 1.0, 0.0).astype(BF16)
    picked = sum(nn(t, picks) for t in split3(sums))
    for i in range(out_ref.shape[0]):
        out_ref[i] = picked[:1]


def local(
    hidden_in, queries, keys_values, attn_out, out_grad, log_norms, proj_in, proj_q, proj_k, proj_v, query_docs
):
    tok = queries.shape[1]
    heads = log_norms.shape[1]
    chips = heads // 2
    docs = lax.axis_size("dp")
    count = query_docs.shape[0]
    same_core = [[2 * p + c for p in range(chips)] for c in range(2)]

    with jax.named_scope("message"):
        msg, proj = message_call(
            hidden_in[0], queries[0], keys_values[0], attn_out[0], out_grad[0], log_norms[0],
            proj_in.T, proj_q.T, proj_k.T, proj_v.T,
        )
    with jax.named_scope("exchange_heads"):
        got = lax.all_to_all(msg, "ctx", 0, 0, axis_index_groups=same_core, tiled=True)
    with jax.named_scope("swap_cores"):
        other = lax.ppermute(keys_call(got), "ctx", [(i, i ^ 1) for i in range(2 * chips)])
    with jax.named_scope("own_keys"):
        saved = own_call(got)
    with jax.named_scope("other_keys"):
        partial = other_call(got, other, proj, saved)
    with jax.named_scope("sum_parts"):
        parts = lax.all_to_all(partial, "ctx", 0, 0, tiled=True)
    with jax.named_scope("unit"):
        unit, mine, send = pl.pallas_call(
            unit_kernel,
            out_shape=(
                jax.ShapeDtypeStruct((RANK, 3 * RANK), F32),
                jax.ShapeDtypeStruct((16, LANES), F32),
                jax.ShapeDtypeStruct((docs, 16, LANES), BF16),
            ),
            in_specs=[VMEM],
            out_specs=(VMEM, VMEM, VMEM),
            scratch_shapes=[pltpu.VMEM((16 * chips, LANES), F32)],
            compiler_params=pltpu.CompilerParams(vmem_limit_bytes=8 * 2**20),
        )(parts)
    with jax.named_scope("exchange_documents"):
        every = lax.all_to_all(send, "dp", 0, 0, tiled=True)
    with jax.named_scope("score"):
        terms = pl.pallas_call(
            score_kernel,
            out_shape=jax.ShapeDtypeStruct((chips, 1, count), F32),
            in_specs=[VMEM] * 3,
            out_specs=VMEM,
            compiler_params=pltpu.CompilerParams(vmem_limit_bytes=8 * 2**20),
        )(query_docs[None], mine, every)
    with jax.named_scope("sum_scores"):
        terms = lax.all_to_all(terms, "ctx", 0, 0, axis_index_groups=same_core, tiled=True)
    scores = jnp.sum(terms, axis=0) / (3.0 * RANK * RANK)
    return (unit.reshape(1, -1), scores)


def solution(mesh):
    in_specs = (
        P("dp", "ctx", None),
        P("dp", "ctx", None),
        P("dp", "ctx", None),
        P("dp", "ctx", None),
        P("dp", "ctx", None),
        P("dp", None, "ctx"),
        P(),
        P(),
        P(),
        P(),
        P(),
    )
    out_specs = (P("dp", None), P("dp", None))
    return jax.shard_map(local, mesh=mesh, in_specs=in_specs, out_specs=out_specs, check_vma=False)
```

```python
import math

import jax
import jax.numpy as jnp
from jax import lax
from jax.experimental import pallas as pl
from jax.experimental.pallas import tpu as pltpu
from jax.sharding import PartitionSpec as P

KV_HEADS = 4
HEAD_DIM = 128
RANK = 64
LANES = 128
SCALE = HEAD_DIM ** (-0.5)
F32 = jnp.float32
BF16 = jnp.bfloat16
VMEM = pl.BlockSpec(memory_space=pltpu.VMEM)
SMEM = pl.BlockSpec(memory_space=pltpu.SMEM)

HBM = pl.BlockSpec(memory_space=pltpu.HBM)

Q_AT, D_AT, V_AT, K_AT, X_AT, WIDE = 0, 256, 512, 640, 768, 896


def nt(a, b):
    return lax.dot_general(a, b, (((1,), (1,)), ((), ())), preferred_element_type=F32)


def tn(a, b):
    return lax.dot_general(a, b, (((0,), (0,)), ((), ())), preferred_element_type=F32)


def nn(a, b):
    return jnp.dot(a, b, preferred_element_type=F32)


def split2(a):
    high = a.astype(BF16)
    return high, (a - high.astype(F32)).astype(BF16)


def lane_of(shape):
    return lax.broadcasted_iota(jnp.int32, shape, len(shape) - 1)


def row_of(shape):
    return lax.broadcasted_iota(jnp.int32, shape, len(shape) - 2)


def place():
    index = lax.axis_index("ctx")
    return lax.div(index, 2), lax.rem(index, 2)


def start_all(pairs, sems):
    copies = [pltpu.make_async_copy(src, dst, sems.at[i]) for i, (src, dst) in enumerate(pairs)]
    for copy in copies:
        copy.start()
    return copies


def row_parts(src, dst, parts):
    rows = src.shape[0] // parts
    return [(src.at[pl.ds(i * rows, rows)], dst.at[pl.ds(i * rows, rows)]) for i in range(parts)]


def message_kernel(
    h_hbm, q_hbm, kv_hbm, o_hbm, d_hbm, lse_hbm, pin_hbm, pq_hbm, pk_hbm, pv_hbm, msg_ref, proj_ref,
    h_ref, kv_ref, o_ref, d_ref, lse_ref, pin_ref, sems,
):
    tok = kv_ref.shape[0]
    heads = lse_ref.shape[0]
    chips = heads // 2
    group = heads // KV_HEADS
    two = 2 * HEAD_DIM
    parts = 2
    chip, _ = place()
    kv_at = head_at(lax.div(2 * chip, group))
    pairs = pl.ds(pl.multiple_of(chip * two, two), two)
    todo = [(pq_hbm.at[:, pairs], proj_ref.at[:, pl.ds(0, two)])]
    todo += [(pk_hbm.at[:, kv_at], proj_ref.at[:, pl.ds(two, HEAD_DIM)])]
    todo += [(pv_hbm.at[:, kv_at], proj_ref.at[:, pl.ds(two + HEAD_DIM, HEAD_DIM)])]
    todo += [(lse_hbm, lse_ref)] + row_parts(d_hbm, d_ref, parts) + row_parts(o_hbm, o_ref, parts)
    deltas = len(todo)
    todo += [(pin_hbm, pin_ref)] + row_parts(h_hbm, h_ref, parts) + row_parts(kv_hbm, kv_ref, parts)
    inputs = len(todo)
    todo += [(q_hbm.at[:, pl.ds(p * two, two)], msg_ref.at[p, :, pl.ds(Q_AT, two)]) for p in range(chips)]
    copies = start_all(todo, sems)
    src = row_of((LANES, chips * LANES))
    dst = lane_of((LANES, chips * LANES))
    head = src % heads
    to = (head // 2) * LANES + RANK + (src // heads) * 6 + (head % 2) * 3
    to = jnp.where(src < 2 * heads, to, -8)
    picks = [jnp.where(dst == to + j, 1.0, 0.0).astype(BF16) for j in range(3)]
    for copy in copies[:deltas]:
        copy.wait()
    lse = jnp.concatenate([lse_ref[...], jnp.zeros((LANES - heads, tok), F32)], axis=0)
    terms = lse.T * (-1.0 / SCALE)
    lane = lane_of((tok, LANES))
    for h in range(heads):
        cols = slice(h * HEAD_DIM, (h + 1) * HEAD_DIM)
        prod = d_ref[:, cols].astype(F32) * o_ref[:, cols].astype(F32)
        delta = jnp.sum(prod, axis=1, keepdims=True)
        terms = jnp.where(lane == heads + h, -delta, terms)
    high = terms.astype(BF16)
    rest = terms - high.astype(F32)
    mid = rest.astype(BF16)
    low = (rest - mid.astype(F32)).astype(BF16)
    spread = nn(high, picks[0]) + nn(mid, picks[1]) + nn(low, picks[2])
    for p in range(chips):
        msg_ref[p, :, D_AT:V_AT] = d_ref[:, p * two : (p + 1) * two]
    for copy in copies[deltas:inputs]:
        copy.wait()
    x = nt(h_ref[...], pin_ref[...])
    x = jnp.concatenate([x, jnp.zeros((tok, LANES - RANK), F32)], axis=1)
    kv_cols = KV_HEADS * HEAD_DIM
    for p in range(chips):
        kv = 2 * p // group
        msg_ref[p, :, V_AT:K_AT] = kv_ref[:, kv_cols + kv * HEAD_DIM : kv_cols + (kv + 1) * HEAD_DIM]
        msg_ref[p, :, K_AT:X_AT] = kv_ref[:, kv * HEAD_DIM : (kv + 1) * HEAD_DIM]
        block = x + spread[:, p * LANES : (p + 1) * LANES]
        msg_ref[p, :, X_AT:] = block.astype(BF16)
    for copy in copies[inputs:]:
        copy.wait()


def message_call(hidden_in, queries, keys_values, attn_out, out_grad, log_norms, proj_in_t, *proj_t):
    tok = queries.shape[0]
    chips = log_norms.shape[0] // 2
    return pl.pallas_call(
        message_kernel,
        out_shape=(
            jax.ShapeDtypeStruct((chips, tok, WIDE), BF16),
            jax.ShapeDtypeStruct((RANK, 4 * HEAD_DIM), BF16),
        ),
        in_specs=[HBM] * 10,
        out_specs=(VMEM, VMEM),
        scratch_shapes=[
            pltpu.VMEM(a.shape, a.dtype)
            for a in (hidden_in, keys_values, attn_out, out_grad, log_norms, proj_in_t)
        ]
        + [pltpu.SemaphoreType.DMA((13 + chips,))],
        compiler_params=pltpu.CompilerParams(vmem_limit_bytes=16 * 2**20),
    )(
        *[
            pltpu.with_memory_space_constraint(a, pltpu.HBM)
            for a in (hidden_in, queries, keys_values, attn_out, out_grad, log_norms, proj_in_t, *proj_t)
        ]
    )


def part(ref, at):
    return ref[:, :, at : at + LANES].reshape(ref.shape[0] * ref.shape[1], LANES)


def head_at(index):
    return pl.ds(pl.multiple_of(index * HEAD_DIM, HEAD_DIM), HEAD_DIM)


def load_keys(ref, base, kt, vt):
    rows = ref.shape[0] * ref.shape[1]
    for to, at in ((kt, K_AT), (vt, V_AT)):
        to[:LANES, :] = part(ref, at - base).T
        to[LANES:, :] = jnp.ones((LANES, rows), BF16)


def group_terms(g, tok, base, seen_of, qs, ds, keys_ref, kt, vt, ps, dss):
    half = 2 * tok
    upto = (g + 1) * half
    fold = SCALE * math.log2(math.e)
    for n in range(g + 1):
        cols = slice(n * half, (n + 1) * half)
        for h in range(2):
            rr = slice(h * half, (h + 1) * half)
            s = nn(qs[g, rr], kt[:, cols])
            probs = jnp.exp2(s * fold)
            if n == g:
                probs = jnp.where(seen_of(row_of((half, half)), lane_of((half, half))), probs, 0.0)
            dscores = probs * nn(ds[g, rr], vt[:, cols])
            ps[rr, cols] = probs.astype(BF16)
            dss[rr, cols] = dscores.astype(BF16)
    keys = keys_ref[: 2 * (g + 1), :, K_AT - base :].reshape(upto, 2 * LANES)
    return nn(ps[:, :upto], keys[:, LANES:]), nn(dss[:, :upto], keys)


def own_kernel(r_ref, qs, ds, acc, acc_v, kt, vt, ps, dss):
    blocks, tok, _ = r_ref.shape
    rows = blocks * tok
    half = 2 * tok
    groups = rows // half
    lane = lane_of((rows, LANES))
    xl = part(r_ref, X_AT)
    none = jnp.zeros_like(xl)
    load_keys(r_ref, 0, kt, vt)
    for h in range(2):
        for ref, at, kind in ((qs, Q_AT, 0), (ds, D_AT, 1)):
            val = part(r_ref, at + h * LANES)
            start = RANK + kind * 6 + h * 3
            side = jnp.where((lane >= start) & (lane < start + 3), xl, none)
            for g in range(groups):
                ref[g, h * half : (h + 1) * half, :LANES] = val[g * half : (g + 1) * half]
                ref[g, h * half : (h + 1) * half, LANES:] = side[g * half : (g + 1) * half]
    for g in range(groups):
        to = slice(2 * g * half, 2 * (g + 1) * half)
        acc_v[to], acc[to] = group_terms(g, tok, 0, lambda r, c: c <= r, qs, ds, r_ref, kt, vt, ps, dss)


def other_kernel(r_ref, o_ref, proj_ref, qs, ds, acc, acc_v, out_ref, kt, vt, ps, dss, rq, rk, rv):
    _, core = place()
    blocks, tok, _ = r_ref.shape
    rows = blocks * tok
    half = 2 * tok
    groups = rows // half
    load_keys(o_ref, V_AT, kt, vt)

    def seen_of(r, c):
        return (c // tok) < (r // tok) + core

    for g in range(groups):
        to = slice(2 * g * half, 2 * (g + 1) * half)
        for_v, for_qk = group_terms(g, tok, V_AT, seen_of, qs, ds, o_ref, kt, vt, ps, dss)
        for_v, for_qk = for_v + acc_v[to], for_qk + acc[to]
        for ref, val in ((rv, for_v), (rk, for_qk[:, LANES:]), (rq, for_qk[:, :LANES])):
            high, low = split2(val)
            for h in range(2):
                mine = slice(h * half, (h + 1) * half)
                at = slice(h * rows + g * half, h * rows + (g + 1) * half)
                ref[at, :LANES] = high[mine]
                ref[at, LANES:] = low[mine]

    def halves(a):
        return a[:, :LANES] + a[:, LANES:]

    def exact(a, b, product):
        high, low = split2(a)
        return product(high, b) + product(low, b)

    xl = part(r_ref, X_AT)
    zero = jnp.zeros((RANK, LANES), F32)
    out_q = zero
    mk = jnp.zeros((LANES, LANES), F32)
    mv = jnp.zeros((LANES, LANES), F32)
    for h in range(2):
        at = slice(h * rows, (h + 1) * rows)
        mq = halves(tn(xl, rq[at])[:RANK])
        pq = jnp.concatenate([proj_ref[:, h * HEAD_DIM : (h + 1) * HEAD_DIM], zero.astype(BF16)], axis=0)
        out_q = out_q + exact(mq, pq, nt)
        mk = mk + halves(tn(part(r_ref, Q_AT + h * LANES), rk[at]))
        mv = mv + halves(tn(part(r_ref, D_AT + h * LANES), rv[at]))
    mk_high, mk_low = split2(mk)
    mv_high, mv_low = split2(mv)
    pk = proj_ref[:, 2 * HEAD_DIM : 3 * HEAD_DIM]
    pv = proj_ref[:, 3 * HEAD_DIM :]
    tk = nn(pk, mk_high) + nn(pk, mk_low)
    tv = nn(pv, mv_high) + nn(pv, mv_low)
    tk = jnp.concatenate([tk, zero], axis=0).T[:RANK] * SCALE
    tv = jnp.concatenate([tv, zero], axis=0).T[:RANK]
    low_lanes = lane_of((RANK, LANES)) < RANK
    top = jnp.where(low_lanes, out_q * SCALE, pltpu.roll(tk, RANK, 1))
    bottom = jnp.where(low_lanes[: RANK // 2], tv[: RANK // 2], pltpu.roll(tv, RANK, 1)[RANK // 2 :])
    packed = jnp.concatenate([top, bottom], axis=0).astype(BF16)
    for i in range(out_ref.shape[0]):
        out_ref[i] = packed


def keys_kernel(r_ref, out_ref):
    out_ref[...] = r_ref[:, :, V_AT:]


def keys_call(got):
    chips, tok, _ = got.shape
    return pl.pallas_call(
        keys_kernel,
        out_shape=jax.ShapeDtypeStruct((chips, tok, WIDE - V_AT), BF16),
        in_specs=[VMEM],
        out_specs=VMEM,
        compiler_params=pltpu.CompilerParams(vmem_limit_bytes=8 * 2**20),
    )(got)


def attention_scratch(rows, half):
    return [
        pltpu.VMEM((2 * LANES, rows), BF16),
        pltpu.VMEM((2 * LANES, rows), BF16),
        pltpu.VMEM((2 * half, rows), BF16),
        pltpu.VMEM((2 * half, rows), BF16),
    ]


def own_call(got):
    chips, tok, _ = got.shape
    rows = chips * tok
    half = 2 * tok
    groups = rows // half
    return pl.pallas_call(
        own_kernel,
        out_shape=(
            jax.ShapeDtypeStruct((groups, 2 * half, 2 * LANES), BF16),
            jax.ShapeDtypeStruct((groups, 2 * half, 2 * LANES), BF16),
            jax.ShapeDtypeStruct((2 * rows, 2 * LANES), F32),
            jax.ShapeDtypeStruct((2 * rows, LANES), F32),
        ),
        in_specs=[VMEM],
        out_specs=(VMEM,) * 4,
        scratch_shapes=attention_scratch(rows, half),
        compiler_params=pltpu.CompilerParams(vmem_limit_bytes=24 * 2**20),
        cost_estimate=pl.CostEstimate(
            flops=2 * 4 * 2 * rows * rows * 2 * LANES, bytes_accessed=8 * 2**20, transcendentals=rows * rows
        ),
    )(got)


def other_call(got, other, proj, saved):
    chips, tok, _ = got.shape
    rows = chips * tok
    half = 2 * tok
    return pl.pallas_call(
        other_kernel,
        out_shape=jax.ShapeDtypeStruct((2 * chips, 3 * RANK // 2, LANES), BF16),
        in_specs=[VMEM] * 7,
        out_specs=VMEM,
        scratch_shapes=attention_scratch(rows, half) + [pltpu.VMEM((2 * rows, 2 * LANES), BF16)] * 3,
        compiler_params=pltpu.CompilerParams(vmem_limit_bytes=24 * 2**20),
    )(got, other, proj, *saved)


def attention_call(got, other, proj):
    return other_call(got, other, proj, own_call(got))


def unit_kernel(parts_ref, unit_ref, mine_ref, send_ref, flat):
    total = parts_ref[0].astype(F32)
    for i in range(1, parts_ref.shape[0]):
        total = total + parts_ref[i].astype(F32)
    mean = jnp.sum(jnp.sum(total * total, axis=0, keepdims=True), axis=1, keepdims=True) / (3.0 * RANK * RANK)
    unit = total / jnp.sqrt(mean + 1e-6)
    unit_ref[:, :LANES] = unit[:RANK]
    unit_ref[: RANK // 2, LANES:] = unit[RANK:, :RANK]
    unit_ref[RANK // 2 :, LANES:] = unit[RANK:, RANK:]
    chips, depth, _ = flat.shape
    for p in range(chips):
        flat[p] = unit[p * depth : (p + 1) * depth]
    chip, _ = place()
    mine = flat[chip]
    rows = mine_ref.shape[0]
    mine = jnp.concatenate([mine[r : r + rows] for r in range(0, depth, rows)], axis=1)
    mine_ref[...] = mine
    send = mine.astype(BF16)
    for i in range(send_ref.shape[0]):
        send_ref[i] = send


def split3(a):
    high, rest = split2(a)
    rest = a - high.astype(F32)
    mid, low = split2(rest)
    return high, mid, low


def score_kernel(docs_ref, mine_ref, every_ref, out_ref):
    mine = mine_ref[...]
    docs = every_ref.shape[0]
    terms = [jnp.sum(mine * every_ref[e].astype(F32), axis=0, keepdims=True) for e in range(docs)]
    terms = jnp.concatenate(terms, axis=0)
    terms = sum(terms[:, i : i + LANES] for i in range(0, terms.shape[1], LANES))
    ones = jnp.ones((8, LANES), BF16)
    sums = sum(nt(ones, t) for t in split3(terms))
    asked = docs_ref[...]
    picks = jnp.where(row_of((docs, asked.shape[1])) == asked, 1.0, 0.0).astype(BF16)
    picked = sum(nn(t, picks) for t in split3(sums))
    for i in range(out_ref.shape[0]):
        out_ref[i] = picked[:1]


def local(
    hidden_in, queries, keys_values, attn_out, out_grad, log_norms, proj_in, proj_q, proj_k, proj_v, query_docs
):
    tok = queries.shape[1]
    heads = log_norms.shape[1]
    chips = heads // 2
    docs = lax.axis_size("dp")
    count = query_docs.shape[0]
    same_core = [[2 * p + c for p in range(chips)] for c in range(2)]

    with jax.named_scope("message"):
        msg, proj = message_call(
            hidden_in[0], queries[0], keys_values[0], attn_out[0], out_grad[0], log_norms[0],
            proj_in.T, proj_q.T, proj_k.T, proj_v.T,
        )
    with jax.named_scope("exchange_heads"):
        got = lax.all_to_all(msg, "ctx", 0, 0, axis_index_groups=same_core, tiled=True)
    with jax.named_scope("swap_cores"):
        other = lax.ppermute(keys_call(got), "ctx", [(i, i ^ 1) for i in range(2 * chips)])
    with jax.named_scope("own_keys"):
        saved = own_call(got)
    with jax.named_scope("other_keys"):
        partial = other_call(got, other, proj, saved)
    with jax.named_scope("sum_parts"):
        parts = lax.all_to_all(partial, "ctx", 0, 0, tiled=True)
    with jax.named_scope("unit"):
        unit, mine, send = pl.pallas_call(
            unit_kernel,
            out_shape=(
                jax.ShapeDtypeStruct((RANK, 3 * RANK), F32),
                jax.ShapeDtypeStruct((4, 3 * LANES), F32),
                jax.ShapeDtypeStruct((docs, 4, 3 * LANES), BF16),
            ),
            in_specs=[VMEM],
            out_specs=(VMEM, VMEM, VMEM),
            scratch_shapes=[pltpu.VMEM((chips, 12, LANES), F32)],
            compiler_params=pltpu.CompilerParams(vmem_limit_bytes=8 * 2**20),
        )(parts)
    with jax.named_scope("exchange_documents"):
        every = lax.all_to_all(send, "dp", 0, 0, tiled=True)
    with jax.named_scope("score"):
        terms = pl.pallas_call(
            score_kernel,
            out_shape=jax.ShapeDtypeStruct((chips, 1, count), F32),
            in_specs=[VMEM] * 3,
            out_specs=VMEM,
            compiler_params=pltpu.CompilerParams(vmem_limit_bytes=8 * 2**20),
        )(query_docs[None], mine, every)
    with jax.named_scope("sum_scores"):
        terms = lax.all_to_all(terms, "ctx", 0, 0, axis_index_groups=same_core, tiled=True)
    scores = jnp.sum(terms, axis=0) / (3.0 * RANK * RANK)
    return (unit.reshape(1, -1), scores)


def solution(mesh):
    in_specs = (
        P("dp", "ctx", None),
        P("dp", "ctx", None),
        P("dp", "ctx", None),
        P("dp", "ctx", None),
        P("dp", "ctx", None),
        P("dp", None, "ctx"),
        P(),
        P(),
        P(),
        P(),
        P(),
    )
    out_specs = (P("dp", None), P("dp", None))
    return jax.shard_map(local, mesh=mesh, in_specs=in_specs, out_specs=out_specs, check_vma=False)
```

```python
import math

import jax
import jax.numpy as jnp
from jax import lax
from jax.experimental import pallas as pl
from jax.experimental.pallas import tpu as pltpu
from jax.sharding import PartitionSpec as P

KV_HEADS = 4
HEAD_DIM = 128
RANK = 64
LANES = 128
SCALE = HEAD_DIM ** (-0.5)
F32 = jnp.float32
BF16 = jnp.bfloat16
VMEM = pl.BlockSpec(memory_space=pltpu.VMEM)
SMEM = pl.BlockSpec(memory_space=pltpu.SMEM)

HBM = pl.BlockSpec(memory_space=pltpu.HBM)

Q_AT, D_AT, V_AT, K_AT, X_AT, T_AT, TALL = 0, 256, 512, 640, 768, 832, 848


def nt(a, b):
    return lax.dot_general(a, b, (((1,), (1,)), ((), ())), preferred_element_type=F32)


def tn(a, b):
    return lax.dot_general(a, b, (((0,), (0,)), ((), ())), preferred_element_type=F32)


def nn(a, b):
    return jnp.dot(a, b, preferred_element_type=F32)


def split2(a):
    high = a.astype(BF16)
    return high, (a - high.astype(F32)).astype(BF16)


def lane_of(shape):
    return lax.broadcasted_iota(jnp.int32, shape, len(shape) - 1)


def row_of(shape):
    return lax.broadcasted_iota(jnp.int32, shape, len(shape) - 2)


def place():
    index = lax.axis_index("ctx")
    return lax.div(index, 2), lax.rem(index, 2)


def start_all(pairs, sems):
    copies = [pltpu.make_async_copy(src, dst, sems.at[i]) for i, (src, dst) in enumerate(pairs)]
    for copy in copies:
        copy.start()
    return copies


def row_parts(src, dst, parts):
    rows = src.shape[0] // parts
    return [(src.at[pl.ds(i * rows, rows)], dst.at[pl.ds(i * rows, rows)]) for i in range(parts)]


def message_kernel(
    h_hbm, q_hbm, kv_hbm, o_hbm, d_hbm, lse_hbm, pin_hbm, pq_hbm, pk_hbm, pv_hbm, msg_ref, proj_ref,
    h_ref, kv_ref, o_ref, d_ref, lse_ref, pin_ref, sems,
):
    tok = kv_ref.shape[0]
    heads = lse_ref.shape[0]
    chips = heads // 2
    group = heads // KV_HEADS
    two = 2 * HEAD_DIM
    parts = 2
    chip, _ = place()
    kv_at = head_at(lax.div(2 * chip, group))
    pairs = pl.ds(pl.multiple_of(chip * two, two), two)
    todo = [(pq_hbm.at[:, pairs], proj_ref.at[:, pl.ds(0, two)])]
    todo += [(pk_hbm.at[:, kv_at], proj_ref.at[:, pl.ds(two, HEAD_DIM)])]
    todo += [(pv_hbm.at[:, kv_at], proj_ref.at[:, pl.ds(two + HEAD_DIM, HEAD_DIM)])]
    todo += [(lse_hbm, lse_ref)] + row_parts(d_hbm, d_ref, parts) + row_parts(o_hbm, o_ref, parts)
    deltas = len(todo)
    todo += [(pin_hbm, pin_ref)] + row_parts(h_hbm, h_ref, parts) + row_parts(kv_hbm, kv_ref, parts)
    inputs = len(todo)
    for h in range(heads):
        cols = pl.ds(h * HEAD_DIM, HEAD_DIM)
        todo += [(q_hbm.at[:, cols], msg_ref.at[h // 2, pl.ds(Q_AT + (h % 2) * tok, tok), :])]
    copies = start_all(todo, sems)
    for copy in copies[:deltas]:
        copy.wait()
    delta = jnp.zeros((tok, LANES), F32)
    lane = lane_of((tok, LANES))
    for h in range(heads):
        cols = slice(h * HEAD_DIM, (h + 1) * HEAD_DIM)
        prod = d_ref[:, cols].astype(F32) * o_ref[:, cols].astype(F32)
        delta = jnp.where(lane == h, jnp.sum(prod, axis=1, keepdims=True), delta)
    delta = -delta.T
    lse = lse_ref[...] * (-1.0 / SCALE)
    terms = [half[2 * p : 2 * p + 2] for p in range(chips) for half in (lse, delta)]
    terms = jnp.concatenate(terms, axis=0)
    high = terms.astype(BF16).astype(F32)
    mid = (terms - high).astype(BF16).astype(F32)
    low = terms - high - mid
    none = jnp.zeros((4, tok), F32)
    for p in range(chips):
        rows = slice(4 * p, 4 * p + 4)
        block = jnp.concatenate([high[rows], mid[rows], low[rows], none], axis=0)
        msg_ref[p, T_AT:, :] = block.astype(BF16)
        for h in range(2):
            cols = slice((2 * p + h) * HEAD_DIM, (2 * p + h + 1) * HEAD_DIM)
            msg_ref[p, D_AT + h * tok : D_AT + (h + 1) * tok, :] = d_ref[:, cols]
    for copy in copies[deltas:inputs]:
        copy.wait()
    x = nt(h_ref[...], pin_ref[...])
    x = jnp.concatenate([x[: tok // 2], x[tok // 2 :]], axis=1).astype(BF16)
    kv_cols = KV_HEADS * HEAD_DIM
    for p in range(chips):
        kv = 2 * p // group
        msg_ref[p, V_AT:K_AT, :] = kv_ref[:, kv_cols + kv * HEAD_DIM : kv_cols + (kv + 1) * HEAD_DIM]
        msg_ref[p, K_AT:X_AT, :] = kv_ref[:, kv * HEAD_DIM : (kv + 1) * HEAD_DIM]
        msg_ref[p, X_AT:T_AT, :] = x
    for copy in copies[inputs:]:
        copy.wait()


def message_call(hidden_in, queries, keys_values, attn_out, out_grad, log_norms, proj_in_t, *proj_t):
    tok = queries.shape[0]
    chips = log_norms.shape[0] // 2
    return pl.pallas_call(
        message_kernel,
        out_shape=(
            jax.ShapeDtypeStruct((chips, TALL, LANES), BF16),
            jax.ShapeDtypeStruct((RANK, 4 * HEAD_DIM), BF16),
        ),
        in_specs=[HBM] * 10,
        out_specs=(VMEM, VMEM),
        scratch_shapes=[
            pltpu.VMEM(a.shape, a.dtype)
            for a in (hidden_in, keys_values, attn_out, out_grad, log_norms, proj_in_t)
        ]
        + [pltpu.SemaphoreType.DMA((13 + 2 * chips,))],
        compiler_params=pltpu.CompilerParams(vmem_limit_bytes=16 * 2**20),
    )(
        *[
            pltpu.with_memory_space_constraint(a, pltpu.HBM)
            for a in (hidden_in, queries, keys_values, attn_out, out_grad, log_norms, proj_in_t, *proj_t)
        ]
    )


def part(ref, at):
    return ref[:, at : at + LANES, :].reshape(ref.shape[0] * LANES, LANES)


def head_at(index):
    return pl.ds(pl.multiple_of(index * HEAD_DIM, HEAD_DIM), HEAD_DIM)


def load_keys(ref, base, kt, vt, kx):
    rows = ref.shape[0] * LANES
    for to, at in ((kt, K_AT), (vt, V_AT)):
        to[:LANES, :] = part(ref, at - base).T
        to[LANES:, :] = jnp.ones((LANES, rows), BF16)
    kx[:, :LANES] = part(ref, K_AT - base)
    half = LANES // 2
    for b in range(ref.shape[0]):
        x = ref[b, X_AT - base : T_AT - base, :]
        kx[b * LANES : b * LANES + half, LANES:] = x
        kx[b * LANES + half : (b + 1) * LANES, LANES:] = pltpu.roll(x.astype(F32), half, 1).astype(BF16)


def group_terms(g, tok, seen_of, qs, ds, kx, kt, vt, ps, dss):
    half = 2 * tok
    upto = (g + 1) * half
    fold = SCALE * math.log2(math.e)
    for n in range(g + 1):
        cols = slice(n * half, (n + 1) * half)
        for h in range(2):
            rr = slice(h * half, (h + 1) * half)
            s = nn(qs[g, rr], kt[:, cols])
            probs = jnp.exp2(s * fold)
            if n == g:
                probs = jnp.where(seen_of(row_of((half, half)), lane_of((half, half))), probs, 0.0)
            dscores = probs * nn(ds[g, rr], vt[:, cols])
            ps[rr, cols] = probs.astype(BF16)
            dss[rr, cols] = dscores.astype(BF16)
    return nn(ps[:, :upto], kx[:upto, LANES:]), nn(dss[:, :upto], kx[:upto, :])


def own_kernel(r_ref, qs, ds, acc, acc_v, xs, kt, vt, kx, ps, dss):
    blocks = r_ref.shape[0]
    tok = LANES
    rows = blocks * tok
    half = 2 * tok
    groups = rows // half
    load_keys(r_ref, 0, kt, vt, kx)
    xs[...] = kx[:, LANES:]
    lane = lane_of((tok, LANES))
    for b in range(blocks):
        terms = r_ref[b, T_AT:, :].astype(F32)
        terms = jnp.concatenate([terms, jnp.zeros((LANES - terms.shape[0], tok), F32)], axis=0).T
        g, at = b // 2, b % 2 * tok
        for h in range(2):
            to = slice(h * half + at, h * half + at + tok)
            for ref, start, kind in ((qs, Q_AT, 0), (ds, D_AT, 1)):
                mine = (lane % 4 == 2 * kind + h) & (lane < 12)
                ref[g, to, :LANES] = r_ref[b, start + h * tok : start + (h + 1) * tok, :]
                ref[g, to, LANES:] = jnp.where(mine, terms, 0.0).astype(BF16)
    for g in range(groups):
        to = slice(2 * g * half, 2 * (g + 1) * half)
        acc_v[to], acc[to] = group_terms(g, tok, lambda r, c: c <= r, qs, ds, kx, kt, vt, ps, dss)


def other_kernel(r_ref, o_ref, proj_ref, qs, ds, acc, acc_v, xs, out_ref, kt, vt, kx, ps, dss, rq, rk, rv):
    _, core = place()
    tok = LANES
    rows = r_ref.shape[0] * tok
    half = 2 * tok
    groups = rows // half
    load_keys(o_ref, V_AT, kt, vt, kx)

    def seen_of(r, c):
        return (c // tok) < (r // tok) + core

    for g in range(groups):
        to = slice(2 * g * half, 2 * (g + 1) * half)
        for_v, for_qk = group_terms(g, tok, seen_of, qs, ds, kx, kt, vt, ps, dss)
        for_v, for_qk = for_v + acc_v[to], for_qk + acc[to]
        for ref, val in ((rv, for_v), (rk, for_qk[:, LANES:]), (rq, for_qk[:, :LANES])):
            high, low = split2(val)
            for h in range(2):
                mine = slice(h * half, (h + 1) * half)
                at = slice(h * rows + g * half, h * rows + (g + 1) * half)
                ref[at, :LANES] = high[mine]
                ref[at, LANES:] = low[mine]

    def halves(a):
        return a[:, :LANES] + a[:, LANES:]

    def exact(a, b, product):
        high, low = split2(a)
        return product(high, b) + product(low, b)

    xl = xs[...]
    zero = jnp.zeros((RANK, LANES), F32)
    out_q = zero
    mk = jnp.zeros((LANES, LANES), F32)
    mv = jnp.zeros((LANES, LANES), F32)
    for h in range(2):
        at = slice(h * rows, (h + 1) * rows)
        mq = halves(tn(xl, rq[at])[:RANK])
        pq = jnp.concatenate([proj_ref[:, h * HEAD_DIM : (h + 1) * HEAD_DIM], zero.astype(BF16)], axis=0)
        out_q = out_q + exact(mq, pq, nt)
        mk = mk + halves(tn(part(r_ref, Q_AT + h * LANES), rk[at]))
        mv = mv + halves(tn(part(r_ref, D_AT + h * LANES), rv[at]))
    mk_high, mk_low = split2(mk)
    mv_high, mv_low = split2(mv)
    pk = proj_ref[:, 2 * HEAD_DIM : 3 * HEAD_DIM]
    pv = proj_ref[:, 3 * HEAD_DIM :]
    tk = nn(pk, mk_high) + nn(pk, mk_low)
    tv = nn(pv, mv_high) + nn(pv, mv_low)
    tk = jnp.concatenate([tk, zero], axis=0).T[:RANK] * SCALE
    tv = jnp.concatenate([tv, zero], axis=0).T[:RANK]
    low_lanes = lane_of((RANK, LANES)) < RANK
    top = jnp.where(low_lanes, out_q * SCALE, pltpu.roll(tk, RANK, 1))
    bottom = jnp.where(low_lanes[: RANK // 2], tv[: RANK // 2], pltpu.roll(tv, RANK, 1)[RANK // 2 :])
    packed = jnp.concatenate([top, bottom], axis=0).astype(BF16)
    for i in range(out_ref.shape[0]):
        out_ref[i] = packed


def keys_kernel(r_ref, out_ref):
    out_ref[...] = r_ref[:, V_AT:T_AT, :]


def keys_call(got):
    return pl.pallas_call(
        keys_kernel,
        out_shape=jax.ShapeDtypeStruct((got.shape[0], T_AT - V_AT, LANES), BF16),
        in_specs=[VMEM],
        out_specs=VMEM,
        compiler_params=pltpu.CompilerParams(vmem_limit_bytes=8 * 2**20),
    )(got)


def attention_scratch(rows, half):
    return [
        pltpu.VMEM((2 * LANES, rows), BF16),
        pltpu.VMEM((2 * LANES, rows), BF16),
        pltpu.VMEM((rows, 2 * LANES), BF16),
        pltpu.VMEM((2 * half, rows), BF16),
        pltpu.VMEM((2 * half, rows), BF16),
    ]


def own_call(got):
    chips = got.shape[0]
    rows = chips * LANES
    half = 2 * LANES
    groups = rows // half
    return pl.pallas_call(
        own_kernel,
        out_shape=(
            jax.ShapeDtypeStruct((groups, 2 * half, 2 * LANES), BF16),
            jax.ShapeDtypeStruct((groups, 2 * half, 2 * LANES), BF16),
            jax.ShapeDtypeStruct((2 * rows, 2 * LANES), F32),
            jax.ShapeDtypeStruct((2 * rows, LANES), F32),
            jax.ShapeDtypeStruct((rows, LANES), BF16),
        ),
        in_specs=[VMEM],
        out_specs=(VMEM,) * 5,
        scratch_shapes=attention_scratch(rows, half),
        compiler_params=pltpu.CompilerParams(vmem_limit_bytes=24 * 2**20),
        cost_estimate=pl.CostEstimate(
            flops=2 * 4 * 2 * rows * rows * 2 * LANES, bytes_accessed=8 * 2**20, transcendentals=rows * rows
        ),
    )(got)


def other_call(got, other, proj, saved):
    chips = got.shape[0]
    rows = chips * LANES
    half = 2 * LANES
    return pl.pallas_call(
        other_kernel,
        out_shape=jax.ShapeDtypeStruct((2 * chips, 3 * RANK // 2, LANES), BF16),
        in_specs=[VMEM] * 8,
        out_specs=VMEM,
        scratch_shapes=attention_scratch(rows, half) + [pltpu.VMEM((2 * rows, 2 * LANES), BF16)] * 3,
        compiler_params=pltpu.CompilerParams(vmem_limit_bytes=24 * 2**20),
    )(got, other, proj, *saved)


def attention_call(got, other, proj):
    return other_call(got, other, proj, own_call(got))


def unit_kernel(parts_ref, unit_ref, mine_ref, send_ref, flat):
    total = parts_ref[0].astype(F32)
    for i in range(1, parts_ref.shape[0]):
        total = total + parts_ref[i].astype(F32)
    mean = jnp.sum(jnp.sum(total * total, axis=0, keepdims=True), axis=1, keepdims=True) / (3.0 * RANK * RANK)
    unit = total / jnp.sqrt(mean + 1e-6)
    unit_ref[:, :LANES] = unit[:RANK]
    unit_ref[: RANK // 2, LANES:] = unit[RANK:, :RANK]
    unit_ref[RANK // 2 :, LANES:] = unit[RANK:, RANK:]
    chips, depth, _ = flat.shape
    for p in range(chips):
        flat[p] = unit[p * depth : (p + 1) * depth]
    chip, _ = place()
    mine = flat[chip]
    rows = mine_ref.shape[0]
    mine = jnp.concatenate([mine[r : r + rows] for r in range(0, depth, rows)], axis=1)
    mine_ref[...] = mine
    send = mine.astype(BF16)
    for i in range(send_ref.shape[0]):
        send_ref[i] = send


def split3(a):
    high, rest = split2(a)
    rest = a - high.astype(F32)
    mid, low = split2(rest)
    return high, mid, low


def score_kernel(docs_ref, mine_ref, every_ref, out_ref):
    mine = mine_ref[...]
    docs = every_ref.shape[0]
    terms = [jnp.sum(mine * every_ref[e].astype(F32), axis=0, keepdims=True) for e in range(docs)]
    terms = jnp.concatenate(terms, axis=0)
    terms = sum(terms[:, i : i + LANES] for i in range(0, terms.shape[1], LANES))
    ones = jnp.ones((8, LANES), BF16)
    sums = sum(nt(ones, t) for t in split3(terms))
    asked = docs_ref[...]
    picks = jnp.where(row_of((docs, asked.shape[1])) == asked, 1.0, 0.0).astype(BF16)
    picked = sum(nn(t, picks) for t in split3(sums))
    for i in range(out_ref.shape[0]):
        out_ref[i] = picked[:1]


def local(
    hidden_in, queries, keys_values, attn_out, out_grad, log_norms, proj_in, proj_q, proj_k, proj_v, query_docs
):
    tok = queries.shape[1]
    heads = log_norms.shape[1]
    chips = heads // 2
    docs = lax.axis_size("dp")
    count = query_docs.shape[0]
    same_core = [[2 * p + c for p in range(chips)] for c in range(2)]

    with jax.named_scope("message"):
        msg, proj = message_call(
            hidden_in[0], queries[0], keys_values[0], attn_out[0], out_grad[0], log_norms[0],
            proj_in.T, proj_q.T, proj_k.T, proj_v.T,
        )
    with jax.named_scope("exchange_heads"):
        got = lax.all_to_all(msg, "ctx", 0, 0, axis_index_groups=same_core, tiled=True)
    with jax.named_scope("swap_cores"):
        other = lax.ppermute(keys_call(got), "ctx", [(i, i ^ 1) for i in range(2 * chips)])
    with jax.named_scope("own_keys"):
        saved = own_call(got)
    with jax.named_scope("other_keys"):
        partial = other_call(got, other, proj, saved)
    with jax.named_scope("sum_parts"):
        parts = lax.all_to_all(partial, "ctx", 0, 0, tiled=True)
    with jax.named_scope("unit"):
        unit, mine, send = pl.pallas_call(
            unit_kernel,
            out_shape=(
                jax.ShapeDtypeStruct((RANK, 3 * RANK), F32),
                jax.ShapeDtypeStruct((4, 3 * LANES), F32),
                jax.ShapeDtypeStruct((docs, 4, 3 * LANES), BF16),
            ),
            in_specs=[VMEM],
            out_specs=(VMEM, VMEM, VMEM),
            scratch_shapes=[pltpu.VMEM((chips, 12, LANES), F32)],
            compiler_params=pltpu.CompilerParams(vmem_limit_bytes=8 * 2**20),
        )(parts)
    with jax.named_scope("exchange_documents"):
        every = lax.all_to_all(send, "dp", 0, 0, tiled=True)
    with jax.named_scope("score"):
        terms = pl.pallas_call(
            score_kernel,
            out_shape=jax.ShapeDtypeStruct((chips, 1, count), F32),
            in_specs=[VMEM] * 3,
            out_specs=VMEM,
            compiler_params=pltpu.CompilerParams(vmem_limit_bytes=8 * 2**20),
        )(query_docs[None], mine, every)
    with jax.named_scope("sum_scores"):
        terms = lax.all_to_all(terms, "ctx", 0, 0, axis_index_groups=same_core, tiled=True)
    scores = jnp.sum(terms, axis=0) / (3.0 * RANK * RANK)
    return (unit.reshape(1, -1), scores)


def solution(mesh):
    in_specs = (
        P("dp", "ctx", None),
        P("dp", "ctx", None),
        P("dp", "ctx", None),
        P("dp", "ctx", None),
        P("dp", "ctx", None),
        P("dp", None, "ctx"),
        P(),
        P(),
        P(),
        P(),
        P(),
    )
    out_specs = (P("dp", None), P("dp", None))
    return jax.shard_map(local, mesh=mesh, in_specs=in_specs, out_specs=out_specs, check_vma=False)
```

```python
import functools
import math

import jax
import jax.numpy as jnp
from jax import lax
from jax.experimental import pallas as pl
from jax.experimental.pallas import tpu as pltpu
from jax.sharding import PartitionSpec as P

KV_HEADS = 4
HEAD_DIM = 128
RANK = 64
LANES = 128
SCALE = HEAD_DIM ** (-0.5)
F32 = jnp.float32
BF16 = jnp.bfloat16
VMEM = pl.BlockSpec(memory_space=pltpu.VMEM)
SMEM = pl.BlockSpec(memory_space=pltpu.SMEM)

HBM = pl.BlockSpec(memory_space=pltpu.HBM)

Q_AT, D_AT, V_AT, K_AT, X_AT, T_AT, TALL = 0, 256, 512, 640, 768, 832, 848


def nt(a, b):
    return lax.dot_general(a, b, (((1,), (1,)), ((), ())), preferred_element_type=F32)


def tn(a, b):
    return lax.dot_general(a, b, (((0,), (0,)), ((), ())), preferred_element_type=F32)


def nn(a, b):
    return jnp.dot(a, b, preferred_element_type=F32)


def split2(a):
    high = a.astype(BF16)
    return high, (a - high.astype(F32)).astype(BF16)


def lane_of(shape):
    return lax.broadcasted_iota(jnp.int32, shape, len(shape) - 1)


def row_of(shape):
    return lax.broadcasted_iota(jnp.int32, shape, len(shape) - 2)


def place():
    index = lax.axis_index("ctx")
    return lax.div(index, 2), lax.rem(index, 2)


def start_all(pairs, sems):
    copies = [pltpu.make_async_copy(src, dst, sems.at[i]) for i, (src, dst) in enumerate(pairs)]
    for copy in copies:
        copy.start()
    return copies


def row_parts(src, dst, parts):
    rows = src.shape[0] // parts
    return [(src.at[pl.ds(i * rows, rows)], dst.at[pl.ds(i * rows, rows)]) for i in range(parts)]


def message_kernel(
    h_hbm, q_hbm, kv_hbm, o_hbm, d_hbm, lse_hbm, pin_hbm, pq_hbm, pk_hbm, pv_hbm, msg_ref, proj_ref,
    h_ref, kv_ref, o_ref, d_ref, lse_ref, pin_ref, sems,
):
    tok = kv_ref.shape[0]
    heads = lse_ref.shape[0]
    chips = heads // 2
    group = heads // KV_HEADS
    two = 2 * HEAD_DIM
    parts = 2
    chip, _ = place()
    kv_at = head_at(lax.div(2 * chip, group))
    pairs = pl.ds(pl.multiple_of(chip * two, two), two)
    todo = [(pq_hbm.at[:, pairs], proj_ref.at[:, pl.ds(0, two)])]
    todo += [(pk_hbm.at[:, kv_at], proj_ref.at[:, pl.ds(two, HEAD_DIM)])]
    todo += [(pv_hbm.at[:, kv_at], proj_ref.at[:, pl.ds(two + HEAD_DIM, HEAD_DIM)])]
    todo += [(lse_hbm, lse_ref)] + row_parts(d_hbm, d_ref, parts) + row_parts(o_hbm, o_ref, parts)
    deltas = len(todo)
    todo += [(pin_hbm, pin_ref)] + row_parts(h_hbm, h_ref, parts) + row_parts(kv_hbm, kv_ref, parts)
    inputs = len(todo)
    for h in range(heads):
        cols = pl.ds(h * HEAD_DIM, HEAD_DIM)
        todo += [(q_hbm.at[:, cols], msg_ref.at[h // 2, pl.ds(Q_AT + (h % 2) * tok, tok), :])]
    copies = start_all(todo, sems)
    for copy in copies[:deltas]:
        copy.wait()
    delta = jnp.zeros((tok, LANES), F32)
    lane = lane_of((tok, LANES))
    for h in range(heads):
        cols = slice(h * HEAD_DIM, (h + 1) * HEAD_DIM)
        prod = d_ref[:, cols].astype(F32) * o_ref[:, cols].astype(F32)
        delta = jnp.where(lane == h, jnp.sum(prod, axis=1, keepdims=True), delta)
    delta = -delta.T
    lse = lse_ref[...] * (-1.0 / SCALE)
    terms = [half[2 * p : 2 * p + 2] for p in range(chips) for half in (lse, delta)]
    terms = jnp.concatenate(terms, axis=0)
    high = terms.astype(BF16).astype(F32)
    mid = (terms - high).astype(BF16).astype(F32)
    low = terms - high - mid
    none = jnp.zeros((4, tok), F32)
    for p in range(chips):
        rows = slice(4 * p, 4 * p + 4)
        block = jnp.concatenate([high[rows], mid[rows], low[rows], none], axis=0)
        msg_ref[p, T_AT:, :] = block.astype(BF16)
        for h in range(2):
            cols = slice((2 * p + h) * HEAD_DIM, (2 * p + h + 1) * HEAD_DIM)
            msg_ref[p, D_AT + h * tok : D_AT + (h + 1) * tok, :] = d_ref[:, cols]
    for copy in copies[deltas:inputs]:
        copy.wait()
    x = nt(h_ref[...], pin_ref[...])
    x = jnp.concatenate([x[: tok // 2], x[tok // 2 :]], axis=1).astype(BF16)
    kv_cols = KV_HEADS * HEAD_DIM
    for p in range(chips):
        kv = 2 * p // group
        msg_ref[p, V_AT:K_AT, :] = kv_ref[:, kv_cols + kv * HEAD_DIM : kv_cols + (kv + 1) * HEAD_DIM]
        msg_ref[p, K_AT:X_AT, :] = kv_ref[:, kv * HEAD_DIM : (kv + 1) * HEAD_DIM]
        msg_ref[p, X_AT:T_AT, :] = x
    for copy in copies[inputs:]:
        copy.wait()


def message_call(hidden_in, queries, keys_values, attn_out, out_grad, log_norms, proj_in_t, *proj_t):
    tok = queries.shape[0]
    chips = log_norms.shape[0] // 2
    return pl.pallas_call(
        message_kernel,
        out_shape=(
            jax.ShapeDtypeStruct((chips, TALL, LANES), BF16),
            jax.ShapeDtypeStruct((RANK, 4 * HEAD_DIM), BF16),
        ),
        in_specs=[HBM] * 10,
        out_specs=(VMEM, VMEM),
        scratch_shapes=[
            pltpu.VMEM(a.shape, a.dtype)
            for a in (hidden_in, keys_values, attn_out, out_grad, log_norms, proj_in_t)
        ]
        + [pltpu.SemaphoreType.DMA((13 + 2 * chips,))],
        compiler_params=pltpu.CompilerParams(vmem_limit_bytes=16 * 2**20),
    )(
        *[
            pltpu.with_memory_space_constraint(a, pltpu.HBM)
            for a in (hidden_in, queries, keys_values, attn_out, out_grad, log_norms, proj_in_t, *proj_t)
        ]
    )


def part(ref, at):
    return ref[:, at : at + LANES, :].reshape(ref.shape[0] * LANES, LANES)


def head_at(index):
    return pl.ds(pl.multiple_of(index * HEAD_DIM, HEAD_DIM), HEAD_DIM)


def load_keys(ref, base, kt, vt, kx):
    rows = ref.shape[0] * LANES
    for to, at in ((kt, K_AT), (vt, V_AT)):
        to[:LANES, :] = part(ref, at - base).T
        to[LANES:, :] = jnp.ones((LANES, rows), BF16)
    kx[:, :LANES] = part(ref, K_AT - base)
    half = LANES // 2
    for b in range(ref.shape[0]):
        x = ref[b, X_AT - base : T_AT - base, :]
        kx[b * LANES : b * LANES + half, LANES:] = x
        kx[b * LANES + half : (b + 1) * LANES, LANES:] = pltpu.roll(x.astype(F32), half, 1).astype(BF16)


def group_terms(g, tok, seen_of, qs, ds, kx, kt, vt, ps, dss):
    half = 2 * tok
    upto = (g + 1) * half
    fold = SCALE * math.log2(math.e)
    for n in range(g + 1):
        cols = slice(n * half, (n + 1) * half)
        for h in range(2):
            rr = slice(h * half, (h + 1) * half)
            s = nn(qs[g, rr], kt[:, cols])
            probs = jnp.exp2(s * fold)
            if n == g:
                probs = jnp.where(seen_of(row_of((half, half)), lane_of((half, half))), probs, 0.0)
            dscores = probs * nn(ds[g, rr], vt[:, cols])
            ps[rr, cols] = probs.astype(BF16)
            dss[rr, cols] = dscores.astype(BF16)
    return nn(ps[:, :upto], kx[:upto, LANES:]), nn(dss[:, :upto], kx[:upto, :])


def own_kernel(r_ref, qs, ds, acc, acc_v, xs, kt, vt, kx, ps, dss):
    blocks = r_ref.shape[0]
    tok = LANES
    rows = blocks * tok
    half = 2 * tok
    groups = rows // half
    load_keys(r_ref, 0, kt, vt, kx)
    xs[...] = kx[:, LANES:]
    lane = lane_of((tok, LANES))
    for b in range(blocks):
        terms = r_ref[b, T_AT:, :].astype(F32)
        terms = jnp.concatenate([terms, jnp.zeros((LANES - terms.shape[0], tok), F32)], axis=0).T
        g, at = b // 2, b % 2 * tok
        for h in range(2):
            to = slice(h * half + at, h * half + at + tok)
            for ref, start, kind in ((qs, Q_AT, 0), (ds, D_AT, 1)):
                mine = (lane % 4 == 2 * kind + h) & (lane < 12)
                ref[g, to, :LANES] = r_ref[b, start + h * tok : start + (h + 1) * tok, :]
                ref[g, to, LANES:] = jnp.where(mine, terms, 0.0).astype(BF16)
    for g in range(groups):
        to = slice(2 * g * half, 2 * (g + 1) * half)
        acc_v[to], acc[to] = group_terms(g, tok, lambda r, c: c <= r, qs, ds, kx, kt, vt, ps, dss)


def other_kernel(r_ref, o_ref, proj_ref, qs, ds, acc, acc_v, xs, out_ref, kt, vt, kx, ps, dss, rq, rk, rv, flat):
    _, core = place()
    tok = LANES
    rows = r_ref.shape[0] * tok
    half = 2 * tok
    groups = rows // half
    load_keys(o_ref, V_AT, kt, vt, kx)

    def seen_of(r, c):
        return (c // tok) < (r // tok) + core

    for g in range(groups):
        to = slice(2 * g * half, 2 * (g + 1) * half)
        for_v, for_qk = group_terms(g, tok, seen_of, qs, ds, kx, kt, vt, ps, dss)
        for_v, for_qk = for_v + acc_v[to], for_qk + acc[to]
        for ref, val in ((rv, for_v), (rk, for_qk[:, LANES:]), (rq, for_qk[:, :LANES])):
            high, low = split2(val)
            for h in range(2):
                mine = slice(h * half, (h + 1) * half)
                at = slice(h * rows + g * half, h * rows + (g + 1) * half)
                ref[at, :LANES] = high[mine]
                ref[at, LANES:] = low[mine]

    def halves(a):
        return a[:, :LANES] + a[:, LANES:]

    def exact(a, b, product):
        high, low = split2(a)
        return product(high, b) + product(low, b)

    xl = xs[...]
    zero = jnp.zeros((RANK, LANES), F32)
    out_q = zero
    mk = jnp.zeros((LANES, LANES), F32)
    mv = jnp.zeros((LANES, LANES), F32)
    for h in range(2):
        at = slice(h * rows, (h + 1) * rows)
        mq = halves(tn(xl, rq[at])[:RANK])
        pq = jnp.concatenate([proj_ref[:, h * HEAD_DIM : (h + 1) * HEAD_DIM], zero.astype(BF16)], axis=0)
        out_q = out_q + exact(mq, pq, nt)
        mk = mk + halves(tn(part(r_ref, Q_AT + h * LANES), rk[at]))
        mv = mv + halves(tn(part(r_ref, D_AT + h * LANES), rv[at]))
    mk_high, mk_low = split2(mk)
    mv_high, mv_low = split2(mv)
    pk = proj_ref[:, 2 * HEAD_DIM : 3 * HEAD_DIM]
    pv = proj_ref[:, 3 * HEAD_DIM :]
    tk = nn(pk, mk_high) + nn(pk, mk_low)
    tv = nn(pv, mv_high) + nn(pv, mv_low)
    tk = jnp.concatenate([tk, zero], axis=0).T[:RANK] * SCALE
    tv = jnp.concatenate([tv, zero], axis=0).T[:RANK]
    low_lanes = lane_of((RANK, LANES)) < RANK
    top = jnp.where(low_lanes, out_q * SCALE, pltpu.roll(tk, RANK, 1))
    flat[:RANK] = top
    flat[RANK : 2 * RANK] = tv
    rows = RANK // 2
    low_lanes = low_lanes[:rows]
    even, odd = flat[pl.ds(0, rows, stride=2), :], flat[pl.ds(1, rows, stride=2), :]
    even_v, odd_v = flat[pl.ds(RANK, rows, stride=2), :], flat[pl.ds(RANK + 1, rows, stride=2), :]
    odd = pltpu.roll(odd, RANK, 1)
    flat[pl.ds(0, rows, stride=3), :] = even
    flat[pl.ds(1, rows, stride=3), :] = jnp.where(low_lanes, even_v, odd)
    flat[pl.ds(2, rows, stride=3), :] = jnp.where(low_lanes, odd, pltpu.roll(odd_v, RANK, 1))
    depth = out_ref.shape[1]
    for i in range(out_ref.shape[0]):
        out_ref[i] = flat[i * depth : (i + 1) * depth]


def keys_kernel(r_ref, out_ref):
    out_ref[...] = r_ref[:, V_AT:T_AT, :]


def keys_call(got):
    return pl.pallas_call(
        keys_kernel,
        out_shape=jax.ShapeDtypeStruct((got.shape[0], T_AT - V_AT, LANES), BF16),
        in_specs=[VMEM],
        out_specs=VMEM,
        compiler_params=pltpu.CompilerParams(vmem_limit_bytes=8 * 2**20),
    )(got)


def attention_scratch(rows, half):
    return [
        pltpu.VMEM((2 * LANES, rows), BF16),
        pltpu.VMEM((2 * LANES, rows), BF16),
        pltpu.VMEM((rows, 2 * LANES), BF16),
        pltpu.VMEM((2 * half, rows), BF16),
        pltpu.VMEM((2 * half, rows), BF16),
    ]


def own_call(got):
    chips = got.shape[0]
    rows = chips * LANES
    half = 2 * LANES
    groups = rows // half
    return pl.pallas_call(
        own_kernel,
        out_shape=(
            jax.ShapeDtypeStruct((groups, 2 * half, 2 * LANES), BF16),
            jax.ShapeDtypeStruct((groups, 2 * half, 2 * LANES), BF16),
            jax.ShapeDtypeStruct((2 * rows, 2 * LANES), F32),
            jax.ShapeDtypeStruct((2 * rows, LANES), F32),
            jax.ShapeDtypeStruct((rows, LANES), BF16),
        ),
        in_specs=[VMEM],
        out_specs=(VMEM,) * 5,
        scratch_shapes=attention_scratch(rows, half),
        compiler_params=pltpu.CompilerParams(vmem_limit_bytes=24 * 2**20),
        cost_estimate=pl.CostEstimate(
            flops=2 * 4 * 2 * rows * rows * 2 * LANES, bytes_accessed=8 * 2**20, transcendentals=rows * rows
        ),
    )(got)


def other_call(got, other, proj, saved):
    chips = got.shape[0]
    rows = chips * LANES
    half = 2 * LANES
    return pl.pallas_call(
        other_kernel,
        out_shape=jax.ShapeDtypeStruct((2 * chips, 3 * RANK // 2 // (2 * chips), LANES), F32),
        in_specs=[VMEM] * 8,
        out_specs=VMEM,
        scratch_shapes=attention_scratch(rows, half) + [pltpu.VMEM((2 * rows, 2 * LANES), BF16)] * 3
        + [pltpu.VMEM((2 * RANK, LANES), F32)],
        compiler_params=pltpu.CompilerParams(vmem_limit_bytes=24 * 2**20),
    )(got, other, proj, *saved)


def attention_call(got, other, proj):
    return other_call(got, other, proj, own_call(got))


def split3(a):
    high, rest = split2(a)
    rest = a - high.astype(F32)
    mid, low = split2(rest)
    return high, mid, low


def slice_kernel(parts_ref, mine_ref, send_ref):
    mine = parts_ref[0]
    for i in range(1, parts_ref.shape[0]):
        mine = mine + parts_ref[i]
    mine_ref[...] = mine
    rows = send_ref.shape[1]
    wide = [mine[r : r + rows] for r in range(0, mine.shape[0], rows)]
    send = jnp.concatenate(wide, axis=1).astype(BF16)
    for i in range(send_ref.shape[0]):
        send_ref[i] = send


def dot_kernel(mine_ref, every_ref, out_ref):
    docs, rows, _ = every_ref.shape
    mine = mine_ref[...]
    wide = jnp.concatenate([mine[r : r + rows] for r in range(0, mine.shape[0], rows)], axis=1)
    terms, squares = [], []
    for e in range(docs):
        other = every_ref[e].astype(F32)
        for to, product in ((terms, wide * other), (squares, other * other)):
            to.append(jnp.sum(product, axis=0, keepdims=True))
    terms = jnp.concatenate(terms + squares, axis=0)
    terms = sum(terms[:, i : i + LANES] for i in range(0, terms.shape[1], LANES))
    terms = jnp.concatenate([terms, jnp.zeros((LANES - 2 * docs, LANES), F32)], axis=0)
    ones = jnp.ones((8, LANES), BF16)
    sums = sum(nt(ones, t) for t in split3(terms))
    depth = mine.shape[0]
    for i in range(out_ref.shape[0]):
        out_ref[i, :depth] = mine
        out_ref[i, depth:] = sums[: out_ref.shape[1] - depth]


def unit_kernel(docs, all_ref, docs_ref, unit_ref, score_ref):
    count, depth = all_ref.shape[0], unit_ref.shape[0] // all_ref.shape[0]
    size = 3.0 * RANK * RANK
    square = jnp.zeros((depth, LANES), F32)
    sums = jnp.zeros((all_ref.shape[1] - depth, LANES), F32)
    for i in range(count):
        part = all_ref[i]
        square = square + part[:depth] * part[:depth]
        sums = sums + part[depth:]
    mean = jnp.sum(jnp.sum(square, axis=0, keepdims=True), axis=1, keepdims=True) / size
    norm = jnp.sqrt(mean + 1e-6)
    for i in range(count):
        unit_ref[i * depth : (i + 1) * depth] = all_ref[i, :depth] / norm
    sums = sums[:1]
    other = jnp.sqrt(sums[:, docs : 2 * docs] / size + 1e-6)
    factor = 1.0 / (norm * size) * (1.0 / other)
    scores = jnp.where(factor == 0.0, 0.0, sums[:, :docs] * factor)
    asked = docs_ref[...]
    picks = jnp.where(row_of((docs, asked.shape[1])) == asked, 1.0, 0.0).astype(BF16)
    scores = jnp.concatenate([scores, jnp.zeros((7, docs), F32)], axis=0)
    score_ref[...] = sum(nn(t, picks) for t in split3(scores))[:1]


def local(
    hidden_in, queries, keys_values, attn_out, out_grad, log_norms, proj_in, proj_q, proj_k, proj_v, query_docs
):
    tok = queries.shape[1]
    heads = log_norms.shape[1]
    chips = heads // 2
    docs = lax.axis_size("dp")
    same_core = [[2 * p + c for p in range(chips)] for c in range(2)]

    with jax.named_scope("message"):
        msg, proj = message_call(
            hidden_in[0], queries[0], keys_values[0], attn_out[0], out_grad[0], log_norms[0],
            proj_in.T, proj_q.T, proj_k.T, proj_v.T,
        )
    with jax.named_scope("exchange_heads"):
        got = lax.all_to_all(msg, "ctx", 0, 0, axis_index_groups=same_core, tiled=True)
    with jax.named_scope("swap_cores"):
        other = lax.ppermute(keys_call(got), "ctx", [(i, i ^ 1) for i in range(2 * chips)])
    with jax.named_scope("own_keys"):
        saved = own_call(got)
    with jax.named_scope("other_keys"):
        partial = other_call(got, other, proj, saved)
    small = pltpu.CompilerParams(vmem_limit_bytes=8 * 2**20)
    with jax.named_scope("exchange_parts"):
        parts = lax.all_to_all(partial, "ctx", 0, 0, tiled=True)
    with jax.named_scope("sum_parts"):
        depth = partial.shape[1]
        mine, send = pl.pallas_call(
            slice_kernel,
            out_shape=(
                jax.ShapeDtypeStruct((depth, LANES), F32),
                jax.ShapeDtypeStruct((docs, 2, depth // 2 * LANES), BF16),
            ),
            in_specs=[VMEM],
            out_specs=(VMEM, VMEM),
            compiler_params=small,
        )(parts)
    with jax.named_scope("exchange_documents"):
        every = lax.all_to_all(send, "dp", 0, 0, tiled=True)
    with jax.named_scope("dots"):
        terms = pl.pallas_call(
            dot_kernel,
            out_shape=jax.ShapeDtypeStruct((2 * chips, 8, LANES), F32),
            in_specs=[VMEM] * 2,
            out_specs=VMEM,
            compiler_params=small,
        )(mine, every)
    with jax.named_scope("exchange_slices"):
        terms = lax.all_to_all(terms, "ctx", 0, 0, tiled=True)
    with jax.named_scope("unit"):
        unit, scores = pl.pallas_call(
            functools.partial(unit_kernel, docs),
            out_shape=(
                jax.ShapeDtypeStruct((3 * RANK // 2, LANES), F32),
                jax.ShapeDtypeStruct((1, query_docs.shape[0]), F32),
            ),
            in_specs=[VMEM] * 2,
            out_specs=(VMEM, VMEM),
            compiler_params=small,
        )(terms, query_docs[None])
    return (unit.reshape(1, -1), scores)


def solution(mesh):
    in_specs = (
        P("dp", "ctx", None),
        P("dp", "ctx", None),
        P("dp", "ctx", None),
        P("dp", "ctx", None),
        P("dp", "ctx", None),
        P("dp", None, "ctx"),
        P(),
        P(),
        P(),
        P(),
        P(),
    )
    out_specs = (P("dp", None), P("dp", None))
    return jax.shard_map(local, mesh=mesh, in_specs=in_specs, out_specs=out_specs, check_vma=False)
```

```python
import functools
import math

import jax
import jax.numpy as jnp
from jax import lax
from jax.experimental import pallas as pl
from jax.experimental.pallas import tpu as pltpu
from jax.sharding import PartitionSpec as P

KV_HEADS = 4
HEAD_DIM = 128
RANK = 64
LANES = 128
SCALE = HEAD_DIM ** (-0.5)
F32 = jnp.float32
BF16 = jnp.bfloat16
VMEM = pl.BlockSpec(memory_space=pltpu.VMEM)
SMEM = pl.BlockSpec(memory_space=pltpu.SMEM)

HBM = pl.BlockSpec(memory_space=pltpu.HBM)

Q_AT, D_AT, V_AT, K_AT, X_AT, T_AT, TALL = 0, 256, 512, 640, 768, 832, 848


def nt(a, b):
    return lax.dot_general(a, b, (((1,), (1,)), ((), ())), preferred_element_type=F32)


def tn(a, b):
    return lax.dot_general(a, b, (((0,), (0,)), ((), ())), preferred_element_type=F32)


def nn(a, b):
    return jnp.dot(a, b, preferred_element_type=F32)


def split2(a):
    high = a.astype(BF16)
    return high, (a - high.astype(F32)).astype(BF16)


def lane_of(shape):
    return lax.broadcasted_iota(jnp.int32, shape, len(shape) - 1)


def row_of(shape):
    return lax.broadcasted_iota(jnp.int32, shape, len(shape) - 2)


def place():
    index = lax.axis_index("ctx")
    return lax.div(index, 2), lax.rem(index, 2)


def start_all(pairs, sems):
    copies = [pltpu.make_async_copy(src, dst, sems.at[i]) for i, (src, dst) in enumerate(pairs)]
    for copy in copies:
        copy.start()
    return copies


def row_parts(src, dst, parts):
    rows = src.shape[0] // parts
    return [(src.at[pl.ds(i * rows, rows)], dst.at[pl.ds(i * rows, rows)]) for i in range(parts)]


def message_kernel(
    h_hbm, q_hbm, kv_hbm, o_hbm, d_hbm, lse_hbm, pin_hbm, pq_hbm, pk_hbm, pv_hbm, msg_ref, proj_ref,
    h_ref, q_ref, kv_ref, o_ref, d_ref, lse_ref, pin_ref, sems,
):
    tok = kv_ref.shape[0]
    heads = lse_ref.shape[0]
    chips = heads // 2
    group = heads // KV_HEADS
    two = 2 * HEAD_DIM
    parts = 2
    chip, _ = place()
    kv_at = head_at(lax.div(2 * chip, group))
    pairs = pl.ds(pl.multiple_of(chip * two, two), two)
    todo = [(pq_hbm.at[:, pairs], proj_ref.at[:, pl.ds(0, two)])]
    todo += [(pk_hbm.at[:, kv_at], proj_ref.at[:, pl.ds(two, HEAD_DIM)])]
    todo += [(pv_hbm.at[:, kv_at], proj_ref.at[:, pl.ds(two + HEAD_DIM, HEAD_DIM)])]
    todo += [(lse_hbm, lse_ref)] + row_parts(d_hbm, d_ref, parts) + row_parts(o_hbm, o_ref, parts)
    deltas = len(todo)
    todo += [(pin_hbm, pin_ref)] + row_parts(h_hbm, h_ref, parts) + row_parts(kv_hbm, kv_ref, parts)
    inputs = len(todo)
    todo += row_parts(q_hbm, q_ref, parts)
    copies = start_all(todo, sems)
    for copy in copies[:deltas]:
        copy.wait()
    delta = jnp.zeros((tok, LANES), F32)
    lane = lane_of((tok, LANES))
    for h in range(heads):
        cols = slice(h * HEAD_DIM, (h + 1) * HEAD_DIM)
        prod = d_ref[:, cols].astype(F32) * o_ref[:, cols].astype(F32)
        delta = jnp.where(lane == h, jnp.sum(prod, axis=1, keepdims=True), delta)
    delta = -delta.T
    lse = lse_ref[...] * (-1.0 / SCALE)
    terms = [half[2 * p : 2 * p + 2] for p in range(chips) for half in (lse, delta)]
    terms = jnp.concatenate(terms, axis=0)
    high = terms.astype(BF16).astype(F32)
    mid = (terms - high).astype(BF16).astype(F32)
    low = terms - high - mid
    none = jnp.zeros((4, tok), F32)
    for p in range(chips):
        rows = slice(4 * p, 4 * p + 4)
        block = jnp.concatenate([high[rows], mid[rows], low[rows], none], axis=0)
        msg_ref[p, T_AT:, :] = block.astype(BF16)
        for h in range(2):
            cols = slice((2 * p + h) * HEAD_DIM, (2 * p + h + 1) * HEAD_DIM)
            msg_ref[p, D_AT + h * tok : D_AT + (h + 1) * tok, :] = d_ref[:, cols]
    for copy in copies[deltas:inputs]:
        copy.wait()
    x = nt(h_ref[...], pin_ref[...])
    x = jnp.concatenate([x[: tok // 2], x[tok // 2 :]], axis=1).astype(BF16)
    kv_cols = KV_HEADS * HEAD_DIM
    for p in range(chips):
        kv = 2 * p // group
        msg_ref[p, V_AT:K_AT, :] = kv_ref[:, kv_cols + kv * HEAD_DIM : kv_cols + (kv + 1) * HEAD_DIM]
        msg_ref[p, K_AT:X_AT, :] = kv_ref[:, kv * HEAD_DIM : (kv + 1) * HEAD_DIM]
        msg_ref[p, X_AT:T_AT, :] = x
    for copy in copies[inputs:]:
        copy.wait()
    for h in range(heads):
        at = Q_AT + h % 2 * tok
        msg_ref[h // 2, at : at + tok, :] = q_ref[:, h * HEAD_DIM : (h + 1) * HEAD_DIM]


def message_call(hidden_in, queries, keys_values, attn_out, out_grad, log_norms, proj_in_t, *proj_t):
    tok = queries.shape[0]
    chips = log_norms.shape[0] // 2
    return pl.pallas_call(
        message_kernel,
        out_shape=(
            jax.ShapeDtypeStruct((chips, TALL, LANES), BF16),
            jax.ShapeDtypeStruct((RANK, 4 * HEAD_DIM), BF16),
        ),
        in_specs=[HBM] * 10,
        out_specs=(VMEM, VMEM),
        scratch_shapes=[
            pltpu.VMEM(a.shape, a.dtype)
            for a in (hidden_in, queries, keys_values, attn_out, out_grad, log_norms, proj_in_t)
        ]
        + [pltpu.SemaphoreType.DMA((15,))],
        compiler_params=pltpu.CompilerParams(vmem_limit_bytes=16 * 2**20),
    )(
        *[
            pltpu.with_memory_space_constraint(a, pltpu.HBM)
            for a in (hidden_in, queries, keys_values, attn_out, out_grad, log_norms, proj_in_t, *proj_t)
        ]
    )


def part(ref, at):
    return ref[:, at : at + LANES, :].reshape(ref.shape[0] * LANES, LANES)


def head_at(index):
    return pl.ds(pl.multiple_of(index * HEAD_DIM, HEAD_DIM), HEAD_DIM)


def load_keys(ref, base, kt, vt, kx):
    rows = ref.shape[0] * LANES
    for to, at in ((kt, K_AT), (vt, V_AT)):
        to[:LANES, :] = part(ref, at - base).T
        to[LANES:, :] = jnp.ones((LANES, rows), BF16)
    kx[:, :LANES] = part(ref, K_AT - base)
    half = LANES // 2
    for b in range(ref.shape[0]):
        x = ref[b, X_AT - base : T_AT - base, :]
        kx[b * LANES : b * LANES + half, LANES:] = x
        kx[b * LANES + half : (b + 1) * LANES, LANES:] = pltpu.roll(x.astype(F32), half, 1).astype(BF16)


def group_terms(g, tok, seen_of, qs, ds, kx, kt, vt, ps, dss):
    half = 2 * tok
    upto = (g + 1) * half
    fold = SCALE * math.log2(math.e)
    for n in range(g + 1):
        cols = slice(n * half, (n + 1) * half)
        for h in range(2):
            rr = slice(h * half, (h + 1) * half)
            s = nn(qs[g, rr], kt[:, cols])
            probs = jnp.exp2(s * fold)
            if n == g:
                probs = jnp.where(seen_of(row_of((half, half)), lane_of((half, half))), probs, 0.0)
            dscores = probs * nn(ds[g, rr], vt[:, cols])
            ps[rr, cols] = probs.astype(BF16)
            dss[rr, cols] = dscores.astype(BF16)
    return nn(ps[:, :upto], kx[:upto, LANES:]), nn(dss[:, :upto], kx[:upto, :])


def own_kernel(r_ref, qs, ds, acc, acc_v, xs, kt, vt, kx, ps, dss):
    blocks = r_ref.shape[0]
    tok = LANES
    rows = blocks * tok
    half = 2 * tok
    groups = rows // half
    load_keys(r_ref, 0, kt, vt, kx)
    xs[...] = kx[:, LANES:]
    lane = lane_of((tok, LANES))
    for b in range(blocks):
        terms = r_ref[b, T_AT:, :].astype(F32)
        terms = jnp.concatenate([terms, jnp.zeros((LANES - terms.shape[0], tok), F32)], axis=0).T
        g, at = b // 2, b % 2 * tok
        for h in range(2):
            to = slice(h * half + at, h * half + at + tok)
            for ref, start, kind in ((qs, Q_AT, 0), (ds, D_AT, 1)):
                mine = (lane % 4 == 2 * kind + h) & (lane < 12)
                ref[g, to, :LANES] = r_ref[b, start + h * tok : start + (h + 1) * tok, :]
                ref[g, to, LANES:] = jnp.where(mine, terms, 0.0).astype(BF16)
    for g in range(groups):
        to = slice(2 * g * half, 2 * (g + 1) * half)
        acc_v[to], acc[to] = group_terms(g, tok, lambda r, c: c <= r, qs, ds, kx, kt, vt, ps, dss)


def other_kernel(r_ref, o_ref, proj_ref, qs, ds, acc, acc_v, xs, out_ref, kt, vt, kx, ps, dss, rq, rk, rv, flat):
    _, core = place()
    tok = LANES
    rows = r_ref.shape[0] * tok
    half = 2 * tok
    groups = rows // half
    load_keys(o_ref, V_AT, kt, vt, kx)

    def seen_of(r, c):
        return (c // tok) < (r // tok) + core

    for g in range(groups):
        to = slice(2 * g * half, 2 * (g + 1) * half)
        for_v, for_qk = group_terms(g, tok, seen_of, qs, ds, kx, kt, vt, ps, dss)
        for_v, for_qk = for_v + acc_v[to], for_qk + acc[to]
        for ref, val in ((rv, for_v), (rk, for_qk[:, LANES:]), (rq, for_qk[:, :LANES])):
            high, low = split2(val)
            for h in range(2):
                mine = slice(h * half, (h + 1) * half)
                at = slice(h * rows + g * half, h * rows + (g + 1) * half)
                ref[at, :LANES] = high[mine]
                ref[at, LANES:] = low[mine]

    def halves(a):
        return a[:, :LANES] + a[:, LANES:]

    def exact(a, b, product):
        high, low = split2(a)
        return product(high, b) + product(low, b)

    xl = xs[...]
    zero = jnp.zeros((RANK, LANES), F32)
    out_q = zero
    mk = jnp.zeros((LANES, LANES), F32)
    mv = jnp.zeros((LANES, LANES), F32)
    for h in range(2):
        at = slice(h * rows, (h + 1) * rows)
        mq = halves(tn(xl, rq[at])[:RANK])
        pq = jnp.concatenate([proj_ref[:, h * HEAD_DIM : (h + 1) * HEAD_DIM], zero.astype(BF16)], axis=0)
        out_q = out_q + exact(mq, pq, nt)
        mk = mk + halves(tn(part(r_ref, Q_AT + h * LANES), rk[at]))
        mv = mv + halves(tn(part(r_ref, D_AT + h * LANES), rv[at]))
    mk_high, mk_low = split2(mk)
    mv_high, mv_low = split2(mv)
    pk = proj_ref[:, 2 * HEAD_DIM : 3 * HEAD_DIM]
    pv = proj_ref[:, 3 * HEAD_DIM :]
    tk = nn(pk, mk_high) + nn(pk, mk_low)
    tv = nn(pv, mv_high) + nn(pv, mv_low)
    tk = jnp.concatenate([tk, zero], axis=0).T[:RANK] * SCALE
    tv = jnp.concatenate([tv, zero], axis=0).T[:RANK]
    low_lanes = lane_of((RANK, LANES)) < RANK
    top = jnp.where(low_lanes, out_q * SCALE, pltpu.roll(tk, RANK, 1))
    flat[:RANK] = top
    flat[RANK : 2 * RANK] = tv
    rows = RANK // 2
    low_lanes = low_lanes[:rows]
    even, odd = flat[pl.ds(0, rows, stride=2), :], flat[pl.ds(1, rows, stride=2), :]
    even_v, odd_v = flat[pl.ds(RANK, rows, stride=2), :], flat[pl.ds(RANK + 1, rows, stride=2), :]
    odd = pltpu.roll(odd, RANK, 1)
    flat[pl.ds(0, rows, stride=3), :] = even
    flat[pl.ds(1, rows, stride=3), :] = jnp.where(low_lanes, even_v, odd)
    flat[pl.ds(2, rows, stride=3), :] = jnp.where(low_lanes, odd, pltpu.roll(odd_v, RANK, 1))
    depth = out_ref.shape[1]
    blocks = out_ref.shape[2] // LANES
    slices = 3 * RANK // 2 // (depth * blocks)
    for i in range(out_ref.shape[0]):
        for j in range(blocks):
            start = (i % slices * blocks + j) * depth
            out_ref[i, :, j * LANES : (j + 1) * LANES] = flat[start : start + depth]


def keys_kernel(r_ref, out_ref):
    out_ref[...] = r_ref[:, V_AT:T_AT, :]


def keys_call(got):
    return pl.pallas_call(
        keys_kernel,
        out_shape=jax.ShapeDtypeStruct((got.shape[0], T_AT - V_AT, LANES), BF16),
        in_specs=[VMEM],
        out_specs=VMEM,
        compiler_params=pltpu.CompilerParams(vmem_limit_bytes=8 * 2**20),
    )(got)


def attention_scratch(rows, half):
    return [
        pltpu.VMEM((2 * LANES, rows), BF16),
        pltpu.VMEM((2 * LANES, rows), BF16),
        pltpu.VMEM((rows, 2 * LANES), BF16),
        pltpu.VMEM((2 * half, rows), BF16),
        pltpu.VMEM((2 * half, rows), BF16),
    ]


def own_call(got):
    chips = got.shape[0]
    rows = chips * LANES
    half = 2 * LANES
    groups = rows // half
    return pl.pallas_call(
        own_kernel,
        out_shape=(
            jax.ShapeDtypeStruct((groups, 2 * half, 2 * LANES), BF16),
            jax.ShapeDtypeStruct((groups, 2 * half, 2 * LANES), BF16),
            jax.ShapeDtypeStruct((2 * rows, 2 * LANES), F32),
            jax.ShapeDtypeStruct((2 * rows, LANES), F32),
            jax.ShapeDtypeStruct((rows, LANES), BF16),
        ),
        in_specs=[VMEM],
        out_specs=(VMEM,) * 5,
        scratch_shapes=attention_scratch(rows, half),
        compiler_params=pltpu.CompilerParams(vmem_limit_bytes=24 * 2**20),
        cost_estimate=pl.CostEstimate(
            flops=2 * 4 * 2 * rows * rows * 2 * LANES, bytes_accessed=8 * 2**20, transcendentals=rows * rows
        ),
    )(got)


def other_call(got, other, proj, saved):
    chips = got.shape[0]
    rows = chips * LANES
    half = 2 * LANES
    return pl.pallas_call(
        other_kernel,
        out_shape=jax.ShapeDtypeStruct((2 * chips, 4, 3 * RANK // 2 // chips // 4 * LANES), F32),
        in_specs=[VMEM] * 8,
        out_specs=VMEM,
        scratch_shapes=attention_scratch(rows, half) + [pltpu.VMEM((2 * rows, 2 * LANES), BF16)] * 3
        + [pltpu.VMEM((2 * RANK, LANES), F32)],
        compiler_params=pltpu.CompilerParams(vmem_limit_bytes=24 * 2**20),
    )(got, other, proj, *saved)


def attention_call(got, other, proj):
    return other_call(got, other, proj, own_call(got))


def split3(a):
    high, rest = split2(a)
    rest = a - high.astype(F32)
    mid, low = split2(rest)
    return high, mid, low


def slice_kernel(parts_ref, mine_ref, send_ref):
    mine = parts_ref[0]
    for i in range(1, parts_ref.shape[0]):
        mine = mine + parts_ref[i]
    mine_ref[...] = mine
    send = mine.astype(BF16)
    for i in range(send_ref.shape[0]):
        send_ref[i] = send


def dot_kernel(mine_ref, every_ref, out_ref):
    docs, rows, width = every_ref.shape
    mine = mine_ref[...]
    terms, squares = [], []
    for e in range(docs):
        other = every_ref[e].astype(F32)
        for to, product in ((terms, mine * other), (squares, other * other)):
            to.append(jnp.sum(product, axis=0, keepdims=True))
    terms = jnp.concatenate(terms + squares, axis=0)
    terms = sum(terms[:, i : i + LANES] for i in range(0, terms.shape[1], LANES))
    terms = jnp.concatenate([terms, jnp.zeros((LANES - 2 * docs, LANES), F32)], axis=0)
    ones = jnp.ones((8, LANES), BF16)
    sums = sum(nt(ones, t) for t in split3(terms))
    depth = rows * (width // LANES)
    for i in range(out_ref.shape[0]):
        for j in range(width // LANES):
            out_ref[i, j * rows : (j + 1) * rows] = mine[:, j * LANES : (j + 1) * LANES]
        out_ref[i, depth:] = sums[: out_ref.shape[1] - depth]


def unit_kernel(docs, all_ref, docs_ref, unit_ref, score_ref):
    count, depth = all_ref.shape[0], unit_ref.shape[0] // all_ref.shape[0]
    size = 3.0 * RANK * RANK
    square = jnp.zeros((depth, LANES), F32)
    sums = jnp.zeros((all_ref.shape[1] - depth, LANES), F32)
    for i in range(count):
        part = all_ref[i]
        square = square + part[:depth] * part[:depth]
        sums = sums + part[depth:]
    mean = jnp.sum(jnp.sum(square, axis=0, keepdims=True), axis=1, keepdims=True) / size
    norm = jnp.sqrt(mean + 1e-6)
    for i in range(count):
        unit_ref[i * depth : (i + 1) * depth] = all_ref[i, :depth] / norm
    sums = sums[:1]
    other = jnp.sqrt(sums[:, docs : 2 * docs] / size + 1e-6)
    factor = 1.0 / (norm * size) * (1.0 / other)
    scores = jnp.where(factor == 0.0, 0.0, sums[:, :docs] * factor)
    asked = docs_ref[...]
    picks = jnp.where(row_of((docs, asked.shape[1])) == asked, 1.0, 0.0).astype(BF16)
    scores = jnp.concatenate([scores, jnp.zeros((7, docs), F32)], axis=0)
    score_ref[...] = sum(nn(t, picks) for t in split3(scores))[:1]


def local(
    hidden_in, queries, keys_values, attn_out, out_grad, log_norms, proj_in, proj_q, proj_k, proj_v, query_docs
):
    tok = queries.shape[1]
    heads = log_norms.shape[1]
    chips = heads // 2
    docs = lax.axis_size("dp")
    same_x = [[chips * x + i for i in range(chips)] for x in range(2)]
    same_core = [[2 * p + c for p in range(chips)] for c in range(2)]

    with jax.named_scope("message"):
        msg, proj = message_call(
            hidden_in[0], queries[0], keys_values[0], attn_out[0], out_grad[0], log_norms[0],
            proj_in.T, proj_q.T, proj_k.T, proj_v.T,
        )
    with jax.named_scope("exchange_heads"):
        got = lax.all_to_all(msg, "ctx", 0, 0, axis_index_groups=same_core, tiled=True)
    with jax.named_scope("swap_cores"):
        other = lax.ppermute(keys_call(got), "ctx", [(i, i ^ 1) for i in range(2 * chips)])
    with jax.named_scope("own_keys"):
        saved = own_call(got)
    with jax.named_scope("other_keys"):
        partial = other_call(got, other, proj, saved)
    small = pltpu.CompilerParams(vmem_limit_bytes=8 * 2**20)
    with jax.named_scope("exchange_parts"):
        parts = lax.all_to_all(partial, "ctx", 0, 0, tiled=True)
    with jax.named_scope("sum_parts"):
        mine, send = pl.pallas_call(
            slice_kernel,
            out_shape=(
                jax.ShapeDtypeStruct(partial.shape[1:], F32),
                jax.ShapeDtypeStruct((docs, *partial.shape[1:]), BF16),
            ),
            in_specs=[VMEM],
            out_specs=(VMEM, VMEM),
            compiler_params=small,
        )(parts)
    with jax.named_scope("exchange_documents"):
        every = lax.all_to_all(send, "dp", 0, 0, tiled=True)
    with jax.named_scope("dots"):
        terms = pl.pallas_call(
            dot_kernel,
            out_shape=jax.ShapeDtypeStruct((chips, 16, LANES), F32),
            in_specs=[VMEM] * 2,
            out_specs=VMEM,
            compiler_params=small,
        )(mine, every)
    with jax.named_scope("exchange_slices"):
        terms = lax.all_to_all(terms, "ctx", 0, 0, axis_index_groups=same_x, tiled=True)
    with jax.named_scope("unit"):
        unit, scores = pl.pallas_call(
            functools.partial(unit_kernel, docs),
            out_shape=(
                jax.ShapeDtypeStruct((3 * RANK // 2, LANES), F32),
                jax.ShapeDtypeStruct((1, query_docs.shape[0]), F32),
            ),
            in_specs=[VMEM] * 2,
            out_specs=(VMEM, VMEM),
            compiler_params=small,
        )(terms, query_docs[None])
    return (unit.reshape(1, -1), scores)


def solution(mesh):
    in_specs = (
        P("dp", "ctx", None),
        P("dp", "ctx", None),
        P("dp", "ctx", None),
        P("dp", "ctx", None),
        P("dp", "ctx", None),
        P("dp", None, "ctx"),
        P(),
        P(),
        P(),
        P(),
        P(),
    )
    out_specs = (P("dp", None), P("dp", None))
    return jax.shard_map(local, mesh=mesh, in_specs=in_specs, out_specs=out_specs, check_vma=False)
```

```python
import functools
import math

import jax
import jax.numpy as jnp
from jax import lax
from jax.experimental import pallas as pl
from jax.experimental.pallas import tpu as pltpu
from jax.sharding import PartitionSpec as P

KV_HEADS = 4
HEAD_DIM = 128
RANK = 64
LANES = 128
SCALE = HEAD_DIM ** (-0.5)
F32 = jnp.float32
BF16 = jnp.bfloat16
VMEM = pl.BlockSpec(memory_space=pltpu.VMEM)
SMEM = pl.BlockSpec(memory_space=pltpu.SMEM)

HBM = pl.BlockSpec(memory_space=pltpu.HBM)

Q_AT, D_AT, V_AT, K_AT, X_AT, T_AT, TALL = 0, 256, 512, 640, 768, 832, 848


def nt(a, b):
    return lax.dot_general(a, b, (((1,), (1,)), ((), ())), preferred_element_type=F32)


def tn(a, b):
    return lax.dot_general(a, b, (((0,), (0,)), ((), ())), preferred_element_type=F32)


def nn(a, b):
    return jnp.dot(a, b, preferred_element_type=F32)


def split2(a):
    high = a.astype(BF16)
    return high, (a - high.astype(F32)).astype(BF16)


def lane_of(shape):
    return lax.broadcasted_iota(jnp.int32, shape, len(shape) - 1)


def row_of(shape):
    return lax.broadcasted_iota(jnp.int32, shape, len(shape) - 2)


def place():
    index = lax.axis_index("ctx")
    return lax.div(index, 2), lax.rem(index, 2)


def start_all(pairs, sems):
    copies = [pltpu.make_async_copy(src, dst, sems.at[i]) for i, (src, dst) in enumerate(pairs)]
    for copy in copies:
        copy.start()
    return copies


def row_parts(src, dst, parts):
    rows = src.shape[0] // parts
    return [(src.at[pl.ds(i * rows, rows)], dst.at[pl.ds(i * rows, rows)]) for i in range(parts)]


def message_kernel(
    h_hbm, q_hbm, kv_hbm, o_hbm, d_hbm, lse_hbm, pin_hbm, pq_hbm, pk_hbm, pv_hbm, msg_ref, proj_ref,
    h_ref, q_ref, kv_ref, o_ref, d_ref, lse_ref, pin_ref, sems,
):
    tok = kv_ref.shape[0]
    heads = lse_ref.shape[0]
    chips = heads // 2
    group = heads // KV_HEADS
    two = 2 * HEAD_DIM
    parts = 2
    chip, _ = place()
    kv_at = head_at(lax.div(2 * chip, group))
    pairs = pl.ds(pl.multiple_of(chip * two, two), two)
    todo = [(pq_hbm.at[:, pairs], proj_ref.at[:, pl.ds(0, two)])]
    todo += [(pk_hbm.at[:, kv_at], proj_ref.at[:, pl.ds(two, HEAD_DIM)])]
    todo += [(pv_hbm.at[:, kv_at], proj_ref.at[:, pl.ds(two + HEAD_DIM, HEAD_DIM)])]
    todo += [(lse_hbm, lse_ref)] + row_parts(d_hbm, d_ref, parts) + row_parts(o_hbm, o_ref, parts)
    deltas = len(todo)
    todo += [(pin_hbm, pin_ref)] + row_parts(h_hbm, h_ref, parts) + row_parts(kv_hbm, kv_ref, parts)
    inputs = len(todo)
    todo += row_parts(q_hbm, q_ref, parts)
    copies = start_all(todo, sems)
    for copy in copies[:deltas]:
        copy.wait()
    delta = jnp.zeros((tok, LANES), F32)
    lane = lane_of((tok, LANES))
    for h in range(heads):
        cols = slice(h * HEAD_DIM, (h + 1) * HEAD_DIM)
        prod = d_ref[:, cols].astype(F32) * o_ref[:, cols].astype(F32)
        delta = jnp.where(lane == h, jnp.sum(prod, axis=1, keepdims=True), delta)
    delta = -delta.T
    lse = lse_ref[...] * (-1.0 / SCALE)
    terms = [half[2 * p : 2 * p + 2] for p in range(chips) for half in (lse, delta)]
    terms = jnp.concatenate(terms, axis=0)
    high = terms.astype(BF16).astype(F32)
    mid = (terms - high).astype(BF16).astype(F32)
    low = terms - high - mid
    none = jnp.zeros((4, tok), F32)
    for p in range(chips):
        rows = slice(4 * p, 4 * p + 4)
        block = jnp.concatenate([high[rows], mid[rows], low[rows], none], axis=0)
        msg_ref[p, T_AT:, :] = block.astype(BF16)
        for h in range(2):
            cols = slice((2 * p + h) * HEAD_DIM, (2 * p + h + 1) * HEAD_DIM)
            msg_ref[p, D_AT + h * tok : D_AT + (h + 1) * tok, :] = d_ref[:, cols]
    for copy in copies[deltas:inputs]:
        copy.wait()
    x = nt(h_ref[...], pin_ref[...])
    x = jnp.concatenate([x[: tok // 2], x[tok // 2 :]], axis=1).astype(BF16)
    kv_cols = KV_HEADS * HEAD_DIM
    for p in range(chips):
        kv = 2 * p // group
        msg_ref[p, V_AT:K_AT, :] = kv_ref[:, kv_cols + kv * HEAD_DIM : kv_cols + (kv + 1) * HEAD_DIM]
        msg_ref[p, K_AT:X_AT, :] = kv_ref[:, kv * HEAD_DIM : (kv + 1) * HEAD_DIM]
        msg_ref[p, X_AT:T_AT, :] = x
    for copy in copies[inputs:]:
        copy.wait()
    for h in range(heads):
        at = Q_AT + h % 2 * tok
        msg_ref[h // 2, at : at + tok, :] = q_ref[:, h * HEAD_DIM : (h + 1) * HEAD_DIM]


def message_call(hidden_in, queries, keys_values, attn_out, out_grad, log_norms, proj_in_t, *proj_t):
    tok = queries.shape[0]
    chips = log_norms.shape[0] // 2
    return pl.pallas_call(
        message_kernel,
        out_shape=(
            jax.ShapeDtypeStruct((chips, TALL, LANES), BF16),
            jax.ShapeDtypeStruct((RANK, 4 * HEAD_DIM), BF16),
        ),
        in_specs=[HBM] * 10,
        out_specs=(VMEM, VMEM),
        scratch_shapes=[
            pltpu.VMEM(a.shape, a.dtype)
            for a in (hidden_in, queries, keys_values, attn_out, out_grad, log_norms, proj_in_t)
        ]
        + [pltpu.SemaphoreType.DMA((15,))],
        compiler_params=pltpu.CompilerParams(vmem_limit_bytes=16 * 2**20),
    )(
        *[
            pltpu.with_memory_space_constraint(a, pltpu.HBM)
            for a in (hidden_in, queries, keys_values, attn_out, out_grad, log_norms, proj_in_t, *proj_t)
        ]
    )


def part(ref, at):
    return ref[:, at : at + LANES, :].reshape(ref.shape[0] * LANES, LANES)


def head_at(index):
    return pl.ds(pl.multiple_of(index * HEAD_DIM, HEAD_DIM), HEAD_DIM)


def load_keys(ref, base, kt, vt, kx):
    rows = ref.shape[0] * LANES
    for to, at in ((kt, K_AT), (vt, V_AT)):
        to[:LANES, :] = part(ref, at - base).T
        to[LANES:, :] = jnp.ones((LANES, rows), BF16)
    kx[:, :LANES] = part(ref, K_AT - base)
    half = LANES // 2
    for b in range(ref.shape[0]):
        x = ref[b, X_AT - base : T_AT - base, :]
        kx[b * LANES : b * LANES + half, LANES:] = x
        kx[b * LANES + half : (b + 1) * LANES, LANES:] = pltpu.roll(x.astype(F32), half, 1).astype(BF16)


def group_terms(g, tok, seen_of, qs, ds, kx, kt, vt, ps, dss):
    half = 2 * tok
    upto = (g + 1) * half
    fold = SCALE * math.log2(math.e)
    for n in range(g + 1):
        cols = slice(n * half, (n + 1) * half)
        for h in range(2):
            rr = slice(h * half, (h + 1) * half)
            s = nn(qs[g, rr], kt[:, cols])
            probs = jnp.exp2(s * fold)
            if n == g:
                probs = jnp.where(seen_of(row_of((half, half)), lane_of((half, half))), probs, 0.0)
            dscores = probs * nn(ds[g, rr], vt[:, cols])
            ps[rr, cols] = probs.astype(BF16)
            dss[rr, cols] = dscores.astype(BF16)
    return nn(ps[:, :upto], kx[:upto, LANES:]), nn(dss[:, :upto], kx[:upto, :])


def own_kernel(r_ref, qs, ds, acc, acc_v, xs, kt, vt, kx, ps, dss):
    blocks = r_ref.shape[0]
    tok = LANES
    rows = blocks * tok
    half = 2 * tok
    groups = rows // half
    load_keys(r_ref, 0, kt, vt, kx)
    xs[...] = kx[:, LANES:]
    lane = lane_of((tok, LANES))
    for b in range(blocks):
        terms = r_ref[b, T_AT:, :].astype(F32)
        terms = jnp.concatenate([terms, jnp.zeros((LANES - terms.shape[0], tok), F32)], axis=0).T
        g, at = b // 2, b % 2 * tok
        for h in range(2):
            to = slice(h * half + at, h * half + at + tok)
            for ref, start, kind in ((qs, Q_AT, 0), (ds, D_AT, 1)):
                mine = (lane % 4 == 2 * kind + h) & (lane < 12)
                ref[g, to, :LANES] = r_ref[b, start + h * tok : start + (h + 1) * tok, :]
                ref[g, to, LANES:] = jnp.where(mine, terms, 0.0).astype(BF16)
    for g in range(groups):
        to = slice(2 * g * half, 2 * (g + 1) * half)
        acc_v[to], acc[to] = group_terms(g, tok, lambda r, c: c <= r, qs, ds, kx, kt, vt, ps, dss)


def other_kernel(r_ref, o_ref, proj_ref, qs, ds, acc, acc_v, xs, out_ref, kt, vt, kx, ps, dss, rq, rk, rv, flat):
    _, core = place()
    tok = LANES
    rows = r_ref.shape[0] * tok
    half = 2 * tok
    groups = rows // half
    load_keys(o_ref, V_AT, kt, vt, kx)

    def seen_of(r, c):
        return (c // tok) < (r // tok) + core

    for g in range(groups):
        to = slice(2 * g * half, 2 * (g + 1) * half)
        for_v, for_qk = group_terms(g, tok, seen_of, qs, ds, kx, kt, vt, ps, dss)
        for_v, for_qk = for_v + acc_v[to], for_qk + acc[to]
        for ref, val in ((rv, for_v), (rk, for_qk[:, LANES:]), (rq, for_qk[:, :LANES])):
            val = val.astype(BF16)
            for h in range(2):
                mine = slice(h * half, (h + 1) * half)
                at = slice(h * rows + g * half, h * rows + (g + 1) * half)
                ref[at, :] = val[mine]

    def exact(a, b, product):
        high, low = split2(a)
        return product(high, b) + product(low, b)

    xl = xs[...]
    zero = jnp.zeros((RANK, LANES), F32)
    out_q = zero
    mk = jnp.zeros((LANES, LANES), F32)
    mv = jnp.zeros((LANES, LANES), F32)
    for h in range(2):
        at = slice(h * rows, (h + 1) * rows)
        mq = tn(xl, rq[at])[:RANK]
        pq = jnp.concatenate([proj_ref[:, h * HEAD_DIM : (h + 1) * HEAD_DIM], zero.astype(BF16)], axis=0)
        out_q = out_q + exact(mq, pq, nt)
        mk = mk + tn(part(r_ref, Q_AT + h * LANES), rk[at])
        mv = mv + tn(part(r_ref, D_AT + h * LANES), rv[at])
    mk_high, mk_low = split2(mk)
    mv_high, mv_low = split2(mv)
    pk = proj_ref[:, 2 * HEAD_DIM : 3 * HEAD_DIM]
    pv = proj_ref[:, 3 * HEAD_DIM :]
    tk = nn(pk, mk_high) + nn(pk, mk_low)
    tv = nn(pv, mv_high) + nn(pv, mv_low)
    tk = jnp.concatenate([tk, zero], axis=0).T[:RANK] * SCALE
    tv = jnp.concatenate([tv, zero], axis=0).T[:RANK]
    low_lanes = lane_of((RANK, LANES)) < RANK
    top = jnp.where(low_lanes, out_q * SCALE, pltpu.roll(tk, RANK, 1))
    flat[:RANK] = top
    flat[RANK : 2 * RANK] = tv
    rows = RANK // 2
    low_lanes = low_lanes[:rows]
    even, odd = flat[pl.ds(0, rows, stride=2), :], flat[pl.ds(1, rows, stride=2), :]
    even_v, odd_v = flat[pl.ds(RANK, rows, stride=2), :], flat[pl.ds(RANK + 1, rows, stride=2), :]
    odd = pltpu.roll(odd, RANK, 1)
    flat[pl.ds(0, rows, stride=3), :] = even
    flat[pl.ds(1, rows, stride=3), :] = jnp.where(low_lanes, even_v, odd)
    flat[pl.ds(2, rows, stride=3), :] = jnp.where(low_lanes, odd, pltpu.roll(odd_v, RANK, 1))
    depth = out_ref.shape[1]
    blocks = out_ref.shape[2] // LANES
    slices = 3 * RANK // 2 // (depth * blocks)
    for i in range(out_ref.shape[0]):
        for j in range(blocks):
            start = (i % slices * blocks + j) * depth
            out_ref[i, :, j * LANES : (j + 1) * LANES] = flat[start : start + depth].astype(BF16)


def keys_kernel(r_ref, out_ref):
    out_ref[...] = r_ref[:, V_AT:T_AT, :]


def keys_call(got):
    return pl.pallas_call(
        keys_kernel,
        out_shape=jax.ShapeDtypeStruct((got.shape[0], T_AT - V_AT, LANES), BF16),
        in_specs=[VMEM],
        out_specs=VMEM,
        compiler_params=pltpu.CompilerParams(vmem_limit_bytes=8 * 2**20),
    )(got)


def attention_scratch(rows, half):
    return [
        pltpu.VMEM((2 * LANES, rows), BF16),
        pltpu.VMEM((2 * LANES, rows), BF16),
        pltpu.VMEM((rows, 2 * LANES), BF16),
        pltpu.VMEM((2 * half, rows), BF16),
        pltpu.VMEM((2 * half, rows), BF16),
    ]


def own_call(got):
    chips = got.shape[0]
    rows = chips * LANES
    half = 2 * LANES
    groups = rows // half
    return pl.pallas_call(
        own_kernel,
        out_shape=(
            jax.ShapeDtypeStruct((groups, 2 * half, 2 * LANES), BF16),
            jax.ShapeDtypeStruct((groups, 2 * half, 2 * LANES), BF16),
            jax.ShapeDtypeStruct((2 * rows, 2 * LANES), F32),
            jax.ShapeDtypeStruct((2 * rows, LANES), F32),
            jax.ShapeDtypeStruct((rows, LANES), BF16),
        ),
        in_specs=[VMEM],
        out_specs=(VMEM,) * 5,
        scratch_shapes=attention_scratch(rows, half),
        compiler_params=pltpu.CompilerParams(vmem_limit_bytes=24 * 2**20),
        cost_estimate=pl.CostEstimate(
            flops=2 * 4 * 2 * rows * rows * 2 * LANES, bytes_accessed=8 * 2**20, transcendentals=rows * rows
        ),
    )(got)


def other_call(got, other, proj, saved):
    chips = got.shape[0]
    rows = chips * LANES
    half = 2 * LANES
    return pl.pallas_call(
        other_kernel,
        out_shape=jax.ShapeDtypeStruct((2 * chips, 4, 3 * RANK // 2 // chips // 4 * LANES), BF16),
        in_specs=[VMEM] * 8,
        out_specs=VMEM,
        scratch_shapes=attention_scratch(rows, half) + [pltpu.VMEM((2 * rows, LANES), BF16)] * 3
        + [pltpu.VMEM((2 * RANK, LANES), F32)],
        compiler_params=pltpu.CompilerParams(vmem_limit_bytes=24 * 2**20),
    )(got, other, proj, *saved)


def attention_call(got, other, proj):
    return other_call(got, other, proj, own_call(got))


def split3(a):
    high, rest = split2(a)
    rest = a - high.astype(F32)
    mid, low = split2(rest)
    return high, mid, low


def slice_kernel(parts_ref, mine_ref, send_ref):
    mine = parts_ref[0].astype(F32)
    for i in range(1, parts_ref.shape[0]):
        mine = mine + parts_ref[i].astype(F32)
    mine_ref[...] = mine
    send = mine.astype(BF16)
    for i in range(send_ref.shape[0]):
        send_ref[i] = send


def dot_kernel(mine_ref, every_ref, out_ref):
    docs, rows, width = every_ref.shape
    mine = mine_ref[...]
    terms, squares = [], []
    for e in range(docs):
        other = every_ref[e].astype(F32)
        for to, product in ((terms, mine * other), (squares, other * other)):
            to.append(jnp.sum(product, axis=0, keepdims=True))
    terms = jnp.concatenate(terms + squares, axis=0)
    terms = sum(terms[:, i : i + LANES] for i in range(0, terms.shape[1], LANES))
    terms = jnp.concatenate([terms, jnp.zeros((LANES - 2 * docs, LANES), F32)], axis=0)
    ones = jnp.ones((8, LANES), BF16)
    sums = sum(nt(ones, t) for t in split3(terms))
    depth = rows * (width // LANES)
    for i in range(out_ref.shape[0]):
        for j in range(width // LANES):
            out_ref[i, j * rows : (j + 1) * rows] = mine[:, j * LANES : (j + 1) * LANES]
        out_ref[i, depth:] = sums[: out_ref.shape[1] - depth]


def unit_kernel(docs, all_ref, docs_ref, unit_ref, score_ref):
    count, depth = all_ref.shape[0], unit_ref.shape[0] // all_ref.shape[0]
    size = 3.0 * RANK * RANK
    square = jnp.zeros((depth, LANES), F32)
    sums = jnp.zeros((all_ref.shape[1] - depth, LANES), F32)
    for i in range(count):
        part = all_ref[i]
        square = square + part[:depth] * part[:depth]
        sums = sums + part[depth:]
    mean = jnp.sum(jnp.sum(square, axis=0, keepdims=True), axis=1, keepdims=True) / size
    norm = jnp.sqrt(mean + 1e-6)
    for i in range(count):
        unit_ref[i * depth : (i + 1) * depth] = all_ref[i, :depth] / norm
    sums = sums[:1]
    other = jnp.sqrt(sums[:, docs : 2 * docs] / size + 1e-6)
    factor = 1.0 / (norm * size) * (1.0 / other)
    scores = jnp.where(factor == 0.0, 0.0, sums[:, :docs] * factor)
    asked = docs_ref[...]
    picks = jnp.where(row_of((docs, asked.shape[1])) == asked, 1.0, 0.0).astype(BF16)
    scores = jnp.concatenate([scores, jnp.zeros((7, docs), F32)], axis=0)
    score_ref[...] = sum(nn(t, picks) for t in split3(scores))[:1]


def local(
    hidden_in, queries, keys_values, attn_out, out_grad, log_norms, proj_in, proj_q, proj_k, proj_v, query_docs
):
    tok = queries.shape[1]
    heads = log_norms.shape[1]
    chips = heads // 2
    docs = lax.axis_size("dp")
    same_x = [[chips * x + i for i in range(chips)] for x in range(2)]
    same_core = [[2 * p + c for p in range(chips)] for c in range(2)]

    with jax.named_scope("message"):
        msg, proj = message_call(
            hidden_in[0], queries[0], keys_values[0], attn_out[0], out_grad[0], log_norms[0],
            proj_in.T, proj_q.T, proj_k.T, proj_v.T,
        )
    with jax.named_scope("exchange_heads"):
        got = lax.all_to_all(msg, "ctx", 0, 0, axis_index_groups=same_core, tiled=True)
    with jax.named_scope("swap_cores"):
        other = lax.ppermute(keys_call(got), "ctx", [(i, i ^ 1) for i in range(2 * chips)])
    with jax.named_scope("own_keys"):
        saved = own_call(got)
    with jax.named_scope("other_keys"):
        partial = other_call(got, other, proj, saved)
    small = pltpu.CompilerParams(vmem_limit_bytes=8 * 2**20)
    with jax.named_scope("exchange_parts"):
        parts = lax.all_to_all(partial, "ctx", 0, 0, tiled=True)
    with jax.named_scope("sum_parts"):
        mine, send = pl.pallas_call(
            slice_kernel,
            out_shape=(
                jax.ShapeDtypeStruct(partial.shape[1:], F32),
                jax.ShapeDtypeStruct((docs, *partial.shape[1:]), BF16),
            ),
            in_specs=[VMEM],
            out_specs=(VMEM, VMEM),
            compiler_params=small,
        )(parts)
    with jax.named_scope("exchange_documents"):
        every = lax.all_to_all(send, "dp", 0, 0, tiled=True)
    with jax.named_scope("dots"):
        terms = pl.pallas_call(
            dot_kernel,
            out_shape=jax.ShapeDtypeStruct((chips, 16, LANES), F32),
            in_specs=[VMEM] * 2,
            out_specs=VMEM,
            compiler_params=small,
        )(mine, every)
    with jax.named_scope("exchange_slices"):
        terms = lax.all_to_all(terms, "ctx", 0, 0, axis_index_groups=same_x, tiled=True)
    with jax.named_scope("unit"):
        unit, scores = pl.pallas_call(
            functools.partial(unit_kernel, docs),
            out_shape=(
                jax.ShapeDtypeStruct((3 * RANK // 2, LANES), F32),
                jax.ShapeDtypeStruct((1, query_docs.shape[0]), F32),
            ),
            in_specs=[VMEM] * 2,
            out_specs=(VMEM, VMEM),
            compiler_params=small,
        )(terms, query_docs[None])
    return (unit.reshape(1, -1), scores)


def solution(mesh):
    in_specs = (
        P("dp", "ctx", None),
        P("dp", "ctx", None),
        P("dp", "ctx", None),
        P("dp", "ctx", None),
        P("dp", "ctx", None),
        P("dp", None, "ctx"),
        P(),
        P(),
        P(),
        P(),
        P(),
    )
    out_specs = (P("dp", None), P("dp", None))
    return jax.shard_map(local, mesh=mesh, in_specs=in_specs, out_specs=out_specs, check_vma=False)
```
